128 devices in a mesh: pp: 4 (over x), ep: 32 (over z, y, core).
Axes of the slice: x: 4, y: 4, z: 4, core: 2. Of those that a mesh axis runs over, the one named last changes fastest.
Arguments:
- hidden_rows: bfloat16 [4096, 7168], P('ep'), may hold values from -6 to 6
- emb_rows: bfloat16 [4096, 7168], P('ep', 'pp'), may hold values from -4 to 4
- expert_ids: int32 [4096, 2], P('ep'), may hold values from 0 to 31, all different within a row; in each aligned block of 128 rows (0 to 127, 128 to 255, ...) at most 16 rows name the same one
- gate_scores: float32 [4096, 2], P('ep'), may hold values from 0.1 to 1
- gain_hidden: float32 [7168], replicated, may hold values from 0.1 to 1.9
- gain_emb: float32 [7168], replicated, may hold values from 0.1 to 1.9
- gate_weight: bfloat16 [32, 7168, 2048], P('ep', None, 'pp'), may hold values from -0.0625 to 0.0625
- up_weight: bfloat16 [32, 7168, 2048], P('ep', None, 'pp'), may hold values from -0.0625 to 0.0625
- down_weight: bfloat16 [32, 2048, 7168], P('ep', 'pp'), may hold values from -0.125 to 0.125
- output_grad: bfloat16 [4096, 7168], P('ep', 'pp'), may hold values from -0.796875 to 0.796875
Outputs:
- moe_out: bfloat16 [4096, 7168], P('ep', 'pp')
- grad_gate: float32 [4096, 2], P('ep')
- grad_hidden: bfloat16 [4096, 7168], P('ep', 'pp')
- grad_emb: bfloat16 [4096, 7168], P('ep', 'pp')
The draws below stay inside these ranges and needn't reach their ends.
Inputs may be any that keep to these rules, and one draw needn't show every extreme that they name: `expert_ids`: each row names 2 different experts. Among the rows of one device no expert is named more than 16 times, and in every draw some device names some expert exactly 16 times.
All inputs are finite; a program needn't handle non-finite values.
Results may differ from the reference program's by a relative error of at most 0.015.
Values may be sent and summed in bfloat16 or wider, within the bound.
No kernel may reach another device: no remote copies, remote signals or barrier semaphores. Data moves between devices by JAX's collectives and lax.ppermute only.
A program may use at most 128 MiB of HBM per device.

```python
import math
import jax
import jax.numpy as jnp
import numpy as np
from jax import lax

D = 7168
HID = 2048
TOK_DEV = 128
ROUTES = 2
EXPERTS = 32
CAP = 16
SLOTS = 512
TOKENS = 4096
N_PP = 4


def level_of(own_key, extent, shards, least, top_value):
    def one(dim, blocks):
        heights = jax.random.uniform(jax.random.fold_in(jax.random.fold_in(own_key, 6), dim), (blocks,), jnp.float32, least / len(shards), top_value / len(shards))
        return jnp.repeat(jnp.exp(heights), extent[dim] // blocks).reshape((-1,) + (1,) * (len(extent) - dim - 1))

    loudness = one(*shards[0])
    for cut in shards[1:]:
        loudness = loudness * one(*cut)
    return loudness


def deal_out(rng, own, number, rows, amount, top, reach, lean):
    sequence = jax.random.permutation(rng, amount)
    heavy_load, common = portions_of(amount, rows * top, reach, lean, True), portions_of(amount, rows * top, reach, lean, False)
    places = jnp.arange(amount)

    def named(sizes, rotation):
        used = int((sizes > 0).sum())
        fixed = max(1, used // 4)
        shifted = fixed + (places - fixed + rotation * (used - fixed)) % max(1, amount - fixed)
        return jnp.zeros((amount,), jnp.int32).at[sequence[jnp.where(places < fixed, places, shifted)]].set(jnp.asarray(sizes, jnp.int32))

    sizes = jnp.where(number % 4 == 0, named(heavy_load, number // 4), named(common, number - number // 4 - 1))
    mixed = jax.random.permutation(jax.random.fold_in(own, 3), amount)
    giver, receiver = mixed[0:amount // 2 * 2:2], mixed[1:amount // 2 * 2:2]
    room = jnp.minimum(sizes[giver] - 1, reach - sizes[receiver]) // 2
    room = jnp.where((giver == sequence[0]) | (receiver == sequence[0]) | (sizes[receiver] == 0), 0, jnp.maximum(room, 0))
    shifted = jax.random.randint(jax.random.fold_in(own, 4), (amount // 2,), 0, 1 << 20) % (room + 1)
    sizes = sizes.at[giver].add(-shifted).at[receiver].add(shifted)
    items = jnp.searchsorted(jnp.cumsum(sizes), jnp.arange(rows * top), side="right").astype(jnp.int32)
    table = items.reshape(top, rows).T
    table = table[jax.random.permutation(jax.random.fold_in(own, 1), rows)]
    rotation = jax.random.randint(jax.random.fold_in(own, 2), (rows, 1), 0, top)
    return jnp.take_along_axis(table, (jnp.arange(top)[None, :] + rotation) % top, axis=1)


def portions_of(amount, total, bound, slope, full):
    weights = [(1 << 20) // math.isqrt(standing ** slope) + 1 for standing in range(1, amount + 1)]
    largest = bound if full else min(bound, max(-(-total // amount), total * weights[0] // sum(weights)))
    least = 1 if total - largest >= amount - 1 else 0
    counts, spare = [largest] + [least] * (amount - 1), total - largest - least * (amount - 1)
    while spare > 0:
        candidates = [i for i in range(1, amount) if counts[i] < largest] or [i for i in range(1, amount) if counts[i] < bound]
        whole, left = sum([weights[i] for i in candidates]), spare
        for i in candidates:
            more = min(bound - counts[i], max(1, left * weights[i] // whole), spare)
            counts[i] = counts[i] + more
            spare = spare - more
    return np.array(counts)


def centred(stream_key, shape, scale, most, split=(), kind=jnp.bfloat16):
    entries = jax.random.normal(stream_key, shape, jnp.float32) * scale
    if len(split) > 0:
        entries = level_of(stream_key, shape, split, -0.22, 0.18) * entries
    return jnp.clip(entries, min=-most, max=most).astype(kind)


def setup_inputs(seed: int = 0) -> dict:
    streams_of = jax.random.split(jax.random.key(seed), 11)
    hidden_rows = centred(streams_of[0], (TOKENS, D), 1.0, 6.0, ((0, 32),))
    emb_rows = centred(streams_of[1], (TOKENS, D), 0.5, 4.0, ((0, 32), (1, 4)))
    expert_ids_keys = jax.random.split(jax.random.fold_in(streams_of[2], 1), TOKENS // TOK_DEV)
    expert_ids_turns = jax.random.permutation(jax.random.fold_in(streams_of[2], 3), TOKENS // TOK_DEV)
    expert_ids = jax.vmap(lambda own, number: deal_out(jax.random.fold_in(streams_of[2], 2), own, number, TOK_DEV, EXPERTS, ROUTES, CAP, 2))(expert_ids_keys, expert_ids_turns).reshape((TOKENS, ROUTES))
    gate_scores = jnp.clip(jnp.exp(math.log(1.0) - 2.3025851 * jax.random.uniform(streams_of[3], (TOKENS, ROUTES), jnp.float32) ** level_of(streams_of[3], (TOKENS, ROUTES), ((0, 32),), -0.2, 0.2)), 0.1, 1.0)
    gain_hidden = jnp.clip(1.0 + 0.18 * jax.random.normal(streams_of[4], (D,), jnp.float32), 0.1, 1.9)
    gain_emb = jnp.clip(1.0 + 0.18 * jax.random.normal(streams_of[5], (D,), jnp.float32), 0.1, 1.9)
    gate_weight = centred(streams_of[6], (EXPERTS, D, HID), D ** -0.5, 0.0625, ((0, 32), (2, 4)))
    up_weight = centred(streams_of[7], (EXPERTS, D, HID), D ** -0.5, 0.0625, ((0, 32), (2, 4)))
    down_weight = centred(streams_of[8], (EXPERTS, HID, D), HID ** -0.5, 0.125, ((0, 32), (1, 4)))
    output_grad = centred(streams_of[9], (TOKENS, D), 0.1, 0.796875, ((0, 32), (1, 4)))
    return {"hidden_rows": hidden_rows, "emb_rows": emb_rows, "expert_ids": expert_ids, "gate_scores": gate_scores, "gain_hidden": gain_hidden, "gain_emb": gain_emb, "gate_weight": gate_weight, "up_weight": up_weight, "down_weight": down_weight, "output_grad": output_grad}


EPS = 1e-06

def root_mean(values):
    return jnp.sqrt(lax.optimization_barrier(jnp.mean(values * values, axis=-1, keepdims=True)) + EPS)

def rounded(values):
    return lax.optimization_barrier(values.astype(jnp.bfloat16)).astype(jnp.float32)

def expert_pass(operands):
    rows_in, grad_in, gate_mat, up_mat, down_mat = operands
    share = HID // N_PP
    gate_pre = jnp.dot(rows_in, gate_mat, preferred_element_type=jnp.float32)
    up_proj = jnp.dot(rows_in, up_mat, preferred_element_type=jnp.float32)
    sigmoid_g = jax.nn.sigmoid(gate_pre)
    activated = (gate_pre * sigmoid_g * up_proj).astype(jnp.bfloat16)
    grad_inner = jnp.dot(grad_in, down_mat.T, preferred_element_type=jnp.float32)
    grad_gate_pre = (grad_inner * up_proj * sigmoid_g * (1.0 + gate_pre * (1.0 - sigmoid_g))).astype(jnp.bfloat16)
    grad_up = (grad_inner * gate_pre * sigmoid_g).astype(jnp.bfloat16)
    forward_sum = jnp.zeros((rows_in.shape[0], D), jnp.float32)
    backward_sum = jnp.zeros((rows_in.shape[0], D), jnp.float32)
    for section in range(N_PP):
        lower = section * share
        upper = lower + share
        forward_sum = forward_sum + rounded(jnp.dot(activated[:, lower:upper], down_mat[lower:upper], preferred_element_type=jnp.float32))
        block_grad = jnp.dot(grad_gate_pre[:, lower:upper], gate_mat[:, lower:upper].T, preferred_element_type=jnp.float32)
        block_grad = block_grad + jnp.dot(grad_up[:, lower:upper], up_mat[:, lower:upper].T, preferred_element_type=jnp.float32)
        backward_sum = backward_sum + rounded(block_grad)
    return (forward_sum.astype(jnp.bfloat16), backward_sum.astype(jnp.bfloat16))

def reference(hidden_rows, emb_rows, expert_ids, gate_scores, gain_hidden, gain_emb, gate_weight, up_weight, down_weight, output_grad):
    hidden_f = hidden_rows.astype(jnp.float32)
    emb_f = emb_rows.astype(jnp.float32)
    hidden_scale = root_mean(hidden_f)
    emb_scale = root_mean(emb_f)
    mixed_input = (hidden_f / hidden_scale * gain_hidden + emb_f / emb_scale * gain_emb).astype(jnp.bfloat16)
    flat_ids = expert_ids.reshape(-1).astype(jnp.int32)
    onehot = (flat_ids[:, None] == jnp.arange(EXPERTS, dtype=jnp.int32)[None, :]).astype(jnp.int32)
    ranking = (lax.optimization_barrier(jnp.sum(jnp.cumsum(onehot, axis=0) * onehot, axis=1)) - 1).astype(jnp.int32)
    position = (flat_ids * SLOTS + ranking).astype(jnp.int32)
    pair_index = jnp.arange(TOKENS * ROUTES, dtype=jnp.int32)
    slot_token = jnp.full((EXPERTS * SLOTS,), TOKENS, jnp.int32).at[position].set((pair_index // ROUTES).astype(jnp.int32))
    slot_pair = jnp.full((EXPERTS * SLOTS,), TOKENS * ROUTES, jnp.int32).at[position].set(pair_index)
    input_pad = jnp.concatenate([mixed_input, jnp.zeros((1, D), jnp.bfloat16)], axis=0)
    grad_pad = jnp.concatenate([output_grad, jnp.zeros((1, D), jnp.bfloat16)], axis=0)
    score_pad = jnp.concatenate([gate_scores.reshape(-1), jnp.zeros((1,), jnp.float32)], axis=0)
    slot_rows = input_pad[slot_token].reshape(EXPERTS, SLOTS, D)
    slot_grads = (score_pad[slot_pair][:, None] * grad_pad[slot_token].astype(jnp.float32)).astype(jnp.bfloat16).reshape(EXPERTS, SLOTS, D)
    outputs, input_grads = lax.map(expert_pass, (slot_rows, slot_grads, gate_weight, up_weight, down_weight))
    expert_output = outputs.reshape(EXPERTS * SLOTS, D)[position].reshape(TOKENS, ROUTES, D).astype(jnp.float32)
    moe_out = lax.optimization_barrier(jnp.sum(gate_scores[:, :, None] * expert_output, axis=1)).astype(jnp.bfloat16)
    grad_f = output_grad.astype(jnp.float32)
    grad_gate = lax.optimization_barrier(jnp.sum(grad_f[:, None, :] * expert_output, axis=2))
    input_grad = lax.optimization_barrier(jnp.sum(input_grads.reshape(EXPERTS * SLOTS, D)[position].reshape(TOKENS, ROUTES, D).astype(jnp.float32), axis=1))
    hidden_dot = lax.optimization_barrier(jnp.sum(input_grad * gain_hidden * hidden_f, axis=1, keepdims=True))
    emb_dot = lax.optimization_barrier(jnp.sum(input_grad * gain_emb * emb_f, axis=1, keepdims=True))
    grad_hidden = gain_hidden * input_grad / hidden_scale - hidden_f * hidden_dot / (D * hidden_scale * hidden_scale * hidden_scale)
    grad_emb = gain_emb * input_grad / emb_scale - emb_f * emb_dot / (D * emb_scale * emb_scale * emb_scale)
    return (moe_out, grad_gate, grad_hidden.astype(jnp.bfloat16), grad_emb.astype(jnp.bfloat16))
```

```python
import jax
import jax.numpy as jnp
from jax import lax
from jax.experimental import pallas as pl
from jax.experimental.pallas import tpu as pltpu
from jax.sharding import PartitionSpec as P

EPS = 1e-06
BF = jnp.bfloat16
F32 = jnp.float32


def dot(left, right, dims):
    return lax.dot_general(left, right, (dims, ((), ())), preferred_element_type=F32)


def shift(value, step):
    ring = lax.axis_size("pp")
    return lax.ppermute(value, "pp", [(i, (i + step) % ring) for i in range(ring)])


def after(value, *others):
    def nothing(*refs):
        pass

    anywhere = pl.BlockSpec(memory_space=pl.ANY)
    return pl.pallas_call(
        nothing,
        out_shape=jax.ShapeDtypeStruct(value.shape, value.dtype),
        in_specs=[anywhere] * (1 + len(others)),
        out_specs=anywhere,
        input_output_aliases={0: 0},
    )(value, *others)


ANYWHERE = pl.BlockSpec(memory_space=pl.ANY)


def params():
    return pltpu.CompilerParams(vmem_limit_bytes=50 * 1024 * 1024)


def ring_gather(own):
    half = own.shape[0] // 2
    below = shift(own, 1)
    above = shift(own, -1)
    return own, above, below, shift(below[:half], 1), shift(above[half:], -1)


def add_halves(up, down, from_below, from_above, *others):
    rows, width = from_below.shape

    def body(up_ref, down_ref, below_ref, above_ref, *refs):
        up_out, down_out = refs[-2:]
        up_out[...] = (up_ref[...].astype(F32) + below_ref[...].astype(F32)).astype(BF)
        down_out[...] = (down_ref[...].astype(F32) + above_ref[...].astype(F32)).astype(BF)

    block = (rows, width // 2)
    first = pl.BlockSpec(block, lambda i: (0, i))
    last = pl.BlockSpec(block, lambda i: (1, i))
    return pl.pallas_call(
        body,
        grid=(2,),
        out_shape=[jax.ShapeDtypeStruct(up.shape, BF)] * 2,
        in_specs=[first, last, first, first] + [ANYWHERE] * len(others),
        out_specs=[first, last],
        input_output_aliases={0: 0, 1: 1},
        compiler_params=params(),
    )(up, down, from_below, from_above, *others)


def ring_scatter(far_low, far_high, rest, *others):
    from_below = shift(far_low, 1)
    from_above = shift(far_high, -1)
    up, down, own = rest()
    up, down = add_halves(up, down, from_below, from_above, *others)
    parts = (own, shift(up, 1), shift(down, -1))
    return parts, (up, down), (from_below, from_above)


def sum_beside(left, parts, *others):
    count, quarter = left.shape
    blocks = 2
    width = quarter // blocks

    def body(left_ref, a_ref, b_ref, c_ref, *refs):
        out = refs[-1]

        @pl.when(pl.program_id(0) < blocks)
        def _():
            out[...] = left_ref[...]

        @pl.when(pl.program_id(0) >= blocks)
        def _():
            total = a_ref[...].astype(F32) + b_ref[...].astype(F32) + c_ref[...].astype(F32)
            out[...] = total.astype(BF)

    copied = pl.BlockSpec((count, width), lambda i: (0, jnp.minimum(i, blocks - 1)))
    added = pl.BlockSpec((count, width), lambda i: (0, jnp.maximum(i - blocks, 0)))
    return pl.pallas_call(
        body,
        grid=(2 * blocks,),
        out_shape=jax.ShapeDtypeStruct((count, 2 * quarter), BF),
        in_specs=[copied, added, added, added] + [ANYWHERE] * len(others),
        out_specs=pl.BlockSpec((count, width), lambda i: (0, i)),
        compiler_params=params(),
    )(left, *parts, *others)


def row_half(array, part, *others):
    rows, width = array.shape

    def body(array_ref, *refs):
        refs[-1][...] = array_ref[...]

    return pl.pallas_call(
        body,
        grid=(1,),
        out_shape=jax.ShapeDtypeStruct((rows // 2, width), array.dtype),
        in_specs=[pl.BlockSpec((rows // 2, width), lambda i: (part, 0))]
        + [ANYWHERE] * len(others),
        out_specs=pl.BlockSpec((rows // 2, width), lambda i: (0, 0)),
        compiler_params=params(),
    )(array, *others)


def cut_columns(here, array, offset, part, *others):
    rows, width = array.shape
    quarter = width // 4
    steps = 2 if part is None else 1
    first = 0 if part is None else part
    block = rows // 2

    def body(here_ref, array_ref, *refs):
        refs[-1][...] = array_ref[...]

    return pl.pallas_call(
        body,
        grid_spec=pltpu.PrefetchScalarGridSpec(
            num_scalar_prefetch=1,
            grid=(steps,),
            in_specs=[
                pl.BlockSpec((block, quarter), lambda i, here: (i + first, (here[0] + offset) % 4))
            ]
            + [ANYWHERE] * len(others),
            out_specs=pl.BlockSpec((block, quarter), lambda i, here: (i, 0)),
        ),
        out_shape=jax.ShapeDtypeStruct((block * steps, quarter), array.dtype),
        compiler_params=params(),
    )(here, array, *others)


def inner_share(grads, pieces, *others):
    count, quarter = grads.shape
    units = pieces[0].shape[0]
    half = count // 2
    number = len(pieces)

    def body(grads_ref, *refs):
        outs = refs[number + len(others) :]
        shares = [
            dot(grads_ref[...], refs[j][...], ((1,), (1,))).astype(BF) for j in range(number)
        ]
        for i in range(2):

            @pl.when(pl.program_id(0) == i)
            def _():
                for j in range(number):
                    outs[i][:, j * units : (j + 1) * units] = shares[j]

    whole = pl.BlockSpec((units, quarter), lambda i: (0, 0))
    return pl.pallas_call(
        body,
        grid=(2,),
        out_shape=[jax.ShapeDtypeStruct((half, number * units), BF)] * 2,
        in_specs=[pl.BlockSpec((half, quarter), lambda i: (i, 0))]
        + [whole] * number
        + [ANYWHERE] * len(others),
        out_specs=[pl.BlockSpec((half, number * units), lambda i: (0, 0))] * 2,
        compiler_params=params(),
    )(grads, *pieces, *others)


def forward(rows, gate_mat, up_mat, *others):
    count, width = rows.shape
    units = gate_mat.shape[1]
    depth = 1024

    def body(rows_ref, gate_ref, up_ref, *refs):
        gate_out, up_out, act_out = refs[-3:]
        step = pl.program_id(0)

        @pl.when(step == 0)
        def _():
            gate_out[...] = jnp.zeros_like(gate_out)
            up_out[...] = jnp.zeros_like(up_out)

        gate_out[...] += jnp.dot(rows_ref[...], gate_ref[...], preferred_element_type=F32)
        up_out[...] += jnp.dot(rows_ref[...], up_ref[...], preferred_element_type=F32)

        @pl.when(step == pl.num_programs(0) - 1)
        def _():
            gate = gate_out[...]
            act_out[...] = (gate * jax.nn.sigmoid(gate) * up_out[...]).astype(BF)

    whole = pl.BlockSpec((count, units), lambda k: (0, 0))
    weight = pl.BlockSpec((depth, units), lambda k: (k, 0))
    return pl.pallas_call(
        body,
        grid=(width // depth,),
        out_shape=[
            jax.ShapeDtypeStruct((count, units), F32),
            jax.ShapeDtypeStruct((count, units), F32),
            jax.ShapeDtypeStruct((count, units), BF),
        ],
        in_specs=[pl.BlockSpec((count, depth), lambda k: (0, k)), weight, weight]
        + [ANYWHERE] * len(others),
        out_specs=[whole, whole, whole],
        compiler_params=params(),
    )(rows, gate_mat, up_mat, *others)


def backward_far(here, h, gate_pre, up_proj, grad_inner, gate_mat, up_mat, *others):
    count, units = gate_pre.shape
    experts, capacity, _ = grad_inner.shape
    quarter = gate_mat.shape[0] // 4
    block = quarter // 2
    half = count // 2

    def body(here_ref, gate_pre_ref, up_ref, inner_ref, gate_w, up_w, *refs):
        ggp, gup, low, high = refs[-4:]

        @pl.when(pl.program_id(0) == 0)
        def _():
            inner = inner_ref[...].reshape(count, units)
            gate = gate_pre_ref[...]
            sig = jax.nn.sigmoid(gate)
            ggp[...] = (inner * up_ref[...] * sig * (1.0 + gate * (1.0 - sig))).astype(BF)
            gup[...] = (inner * gate * sig).astype(BF)

        piece = dot(ggp[...], gate_w[...], ((1,), (1,))) + dot(gup[...], up_w[...], ((1,), (1,)))
        low[...] = piece[:half].astype(BF)
        high[...] = piece[half:].astype(BF)

    whole = pl.BlockSpec((count, units), lambda j, here: (0, 0))
    weight = pl.BlockSpec((block, units), lambda j, here: (((here[0] + 2) % 4) * 2 + j, 0))
    out = pl.BlockSpec((half, block), lambda j, here: (0, j))
    return pl.pallas_call(
        body,
        grid_spec=pltpu.PrefetchScalarGridSpec(
            num_scalar_prefetch=1,
            grid=(2,),
            in_specs=[
                whole,
                whole,
                pl.BlockSpec((experts, capacity // 2, units), lambda j, here: (0, h, 0)),
                weight,
                weight,
            ]
            + [ANYWHERE] * len(others),
            out_specs=[whole, whole, out, out],
        ),
        out_shape=[
            jax.ShapeDtypeStruct((count, units), BF),
            jax.ShapeDtypeStruct((count, units), BF),
            jax.ShapeDtypeStruct((half, quarter), BF),
            jax.ShapeDtypeStruct((half, quarter), BF),
        ],
        compiler_params=params(),
    )(here, gate_pre, up_proj, grad_inner, gate_mat, up_mat, *others)


def backward_rest(here, grad_gate_pre, grad_up, gate_mat, up_mat):
    count, units = grad_up.shape
    quarter = gate_mat.shape[0] // 4
    block = quarter // 2

    def body(here_ref, ggp, gup, gate_w, up_w, *outs):
        step = pl.program_id(0)
        piece = dot(ggp[...], gate_w[...], ((1,), (1,))) + dot(gup[...], up_w[...], ((1,), (1,)))
        piece = piece.astype(BF)
        for i in range(3):

            @pl.when(step // 2 == i)
            def _():
                outs[i][...] = piece

    whole = pl.BlockSpec((count, units), lambda s, here: (0, 0))

    def weight_block(s, here):
        r = jnp.where(s // 2 == 0, 1, jnp.where(s // 2 == 1, 3, 0))
        return (((here[0] + r) % 4) * 2 + s % 2, 0)

    def out_spec(i):
        return pl.BlockSpec((count, block), lambda s, here: (0, jnp.clip(s - 2 * i, 0, 1)))

    weight = pl.BlockSpec((block, units), weight_block)
    return pl.pallas_call(
        body,
        grid_spec=pltpu.PrefetchScalarGridSpec(
            num_scalar_prefetch=1,
            grid=(6,),
            in_specs=[whole, whole, weight, weight],
            out_specs=[out_spec(i) for i in range(3)],
        ),
        out_shape=[jax.ShapeDtypeStruct((count, quarter), BF) for _ in range(3)],
        compiler_params=params(),
    )(here, grad_gate_pre, grad_up, gate_mat, up_mat)


def down_product(acts, downs, *others):
    count, units = acts[0].shape
    quarter = downs[0].shape[1]
    block = 256
    half_units = units // 2

    def body(a0, a1, a3, a2_low, a2_high, *refs):
        down_refs, (out, far) = refs[: len(downs)], refs[-2:]

        @pl.when(pl.program_id(0) == 0)
        def _():
            far[: count // 2] = a2_low[...]
            far[count // 2 :] = a2_high[...]

        total = jnp.dot(a0[...], down_refs[0][...], preferred_element_type=F32)
        total += jnp.dot(a1[...], down_refs[1][...], preferred_element_type=F32)
        total += jnp.dot(a3[...], down_refs[2][...], preferred_element_type=F32)
        for part in range(2):
            left = far[:, part * half_units : (part + 1) * half_units]
            total += jnp.dot(left, down_refs[3 + part][...], preferred_element_type=F32)
        out[...] = total.astype(BF)

    def held(array):
        return pl.BlockSpec(array.shape, lambda j: (0, 0))

    def streamed(array):
        return pl.BlockSpec((array.shape[0], block), lambda j: (0, j))

    return pl.pallas_call(
        body,
        grid=(quarter // block,),
        out_shape=jax.ShapeDtypeStruct((count, quarter), BF),
        in_specs=[held(a) for a in acts]
        + [streamed(d) for d in downs]
        + [ANYWHERE] * len(others),
        out_specs=pl.BlockSpec((count, block), lambda j: (0, j)),
        scratch_shapes=[pltpu.VMEM((count, units), BF)],
        compiler_params=params(),
    )(*acts, *downs, *others)


def exchange(value):
    return lax.all_to_all(value, "ep", split_axis=0, concat_axis=0, tiled=True)


def per_device(
    hidden_rows,
    emb_rows,
    expert_ids,
    gate_scores,
    gain_hidden,
    gain_emb,
    gate_weight,
    up_weight,
    down_weight,
    output_grad,
):
    tokens, width = hidden_rows.shape
    quarter = emb_rows.shape[1]
    routes = expert_ids.shape[1]
    experts = lax.axis_size("ep")
    ring = lax.axis_size("pp")
    here = lax.axis_index("pp")
    capacity = 2 * tokens * routes // experts
    part = capacity // 2
    gate_mat, up_mat, down_mat = gate_weight[0], up_weight[0], down_weight[0]
    hidden_units = down_mat.shape[0]

    def columns(array, r):
        return lax.dynamic_slice_in_dim(array, ((here + r) % ring) * quarter, quarter, 1)

    flat_ids = expert_ids.reshape(-1)
    onehot = (flat_ids[:, None] == jnp.arange(experts, dtype=jnp.int32)[None, :]).astype(jnp.int32)
    ranking = jnp.sum(jnp.cumsum(onehot, axis=0) * onehot, axis=1) - 1
    ranking = ranking.reshape(tokens, routes)
    slot_ids = expert_ids * capacity + ranking
    slot_range = jnp.arange(experts * capacity, dtype=jnp.int32)
    selectors = [slot_ids[:, k][:, None] == slot_range[None, :] for k in range(routes)]
    placement = (selectors[0] | selectors[1]).astype(BF)
    slot_score = jnp.sum(
        sum(selectors[k].astype(F32) * gate_scores[:, k : k + 1] for k in range(routes)), axis=0
    )
    part_ids = jnp.where(
        ranking < part,
        expert_ids * part + ranking,
        experts * part + expert_ids * part + ranking - part,
    )
    part_range = jnp.arange(experts * part, dtype=jnp.int32)
    part_selectors = [
        [part_ids[:, k][:, None] == (part_range + h * experts * part)[None, :] for k in range(routes)]
        for h in range(2)
    ]
    part_placement = [(part_selectors[h][0] | part_selectors[h][1]).astype(BF) for h in range(2)]

    emb_own, emb_above, emb_below, emb_low, emb_high = ring_gather(emb_rows)
    emb_pieces = [emb_own, emb_above, jnp.concatenate([emb_low, emb_high], axis=0), emb_below]

    place = here.reshape(1)
    down_low, down_high = (cut_columns(place, down_mat, 2, i) for i in range(2))
    pass_low, pass_high = shift(down_low, 1), shift(down_high, -1)
    far_low, far_high = shift(pass_low, 1), shift(pass_high, -1)

    grad_send = (dot(placement, output_grad, ((0,), (0,))) * slot_score[:, None]).astype(BF)
    grad_send = after(grad_send, down_low, down_high)
    grad_slots = exchange(grad_send.reshape(experts, capacity, quarter))
    grad_slots = grad_slots.reshape(experts * capacity, quarter)

    emb_twice = jnp.concatenate(emb_pieces + emb_pieces, axis=1)
    emb_full = lax.dynamic_slice_in_dim(emb_twice, ((ring - here) % ring) * quarter, width, 1)
    hidden_f = hidden_rows.astype(F32)
    emb_f = emb_full.astype(F32)
    hidden_scale = jnp.sqrt(jnp.mean(hidden_f * hidden_f, axis=1, keepdims=True) + EPS)
    emb_scale = jnp.sqrt(jnp.mean(emb_f * emb_f, axis=1, keepdims=True) + EPS)
    mixed_input = (hidden_f / hidden_scale * gain_hidden + emb_f / emb_scale * gain_emb).astype(BF)
    send_rows = [
        dot(part_placement[h], mixed_input, ((0,), (0,))).astype(BF) for h in range(2)
    ]
    down_up = cut_columns(place, down_mat, 1, None, send_rows[0])
    down_back = cut_columns(place, down_mat, 3, None, send_rows[0])
    down_below, down_above = shift(down_up, 1), shift(down_back, -1)
    down_own = cut_columns(place, down_mat, 0, None, grad_slots)
    far = inner_share(grad_slots, (far_low, far_high))
    own = dot(grad_slots, down_own, ((1,), (1,)))
    send_rows[0] = after(send_rows[0], far_low, far_high, down_up, down_back)
    send_rows[1] = after(send_rows[1], down_above, down_below, *far, own)
    arrived = [
        exchange(send_rows[h].reshape(experts, part, width)).reshape(experts * part, width)
        for h in range(2)
    ]
    downs = (down_own, down_above, down_below, far_low, far_high)
    up = jnp.concatenate(inner_share(grad_slots, (down_above,)), axis=0)
    down = jnp.concatenate(inner_share(grad_slots, (down_below,)), axis=0)
    inner_shares, passed, _ = ring_scatter(*far, lambda: (up, down, own))

    gate_pre, up_proj, act = forward(arrived[0], gate_mat, up_mat, *passed)
    act_below, act_above = shift(act, 1), shift(act, -1)
    inner_shares = (after(own, act), *inner_shares[1:])
    grad_inner = sum(share.astype(F32) for share in inner_shares)
    grad_inner = grad_inner.reshape(experts, capacity, hidden_units)
    grad_gate_pre, grad_up, low, high = backward_far(
        place, 0, gate_pre, up_proj, grad_inner, gate_mat, up_mat
    )
    rest = backward_rest(place, grad_gate_pre, grad_up, gate_mat, up_mat)
    act_low = shift(row_half(act_below, 0, rest[0]), 1)
    act_high = shift(row_half(act_above, 1, rest[0]), -1)
    first_acts = (act, act_above, act_below, act_low, act_high)

    gate_pre, up_proj, act = forward(arrived[1], gate_mat, up_mat, rest[0])
    first, passed, _ = ring_scatter(low, high, lambda: rest, act_low, act_high, act)
    act_below, act_above = shift(act, 1), shift(act, -1)
    grad_gate_pre, grad_up, low, high = backward_far(
        place, 1, gate_pre, up_proj, grad_inner, gate_mat, up_mat, *passed
    )
    first_output = down_product(first_acts, downs, low)
    last = backward_rest(place, grad_gate_pre, grad_up, gate_mat, up_mat)
    act_low = shift(row_half(act_below, 0, last[0]), 1)
    act_high = shift(row_half(act_above, 1, last[0]), -1)
    acts = (act, act_above, act_below, act_low, act_high)
    second, passed, came = ring_scatter(low, high, lambda: last, act_low, act_high)
    output = down_product(acts, downs, *passed)

    returned = [
        exchange(both.reshape(experts, part, 2 * quarter))
        for both in (sum_beside(first_output, first, *came), sum_beside(output, second))
    ]
    returned = [both.reshape(experts * part, 2 * quarter) for both in returned]
    back = [both[:, :quarter] for both in returned]
    grads_back = [both[:, quarter:] for both in returned]

    route_outputs = [
        sum(dot(part_selectors[h][k].astype(BF), back[h], ((1,), (0,))) for h in range(2))
        for k in range(routes)
    ]
    moe_out = sum(gate_scores[:, k : k + 1] * route_outputs[k] for k in range(routes)).astype(BF)
    input_grad = sum(dot(part_placement[h], grads_back[h], ((1,), (0,))) for h in range(2))

    grad_f = output_grad.astype(F32)
    hidden_cols = columns(hidden_rows, 0).astype(F32)
    emb_cols = emb_rows.astype(F32)
    gain_hidden_cols = lax.dynamic_slice_in_dim(gain_hidden, here * quarter, quarter, 0)
    gain_emb_cols = lax.dynamic_slice_in_dim(gain_emb, here * quarter, quarter, 0)
    partial = jnp.stack(
        [jnp.sum(grad_f * route_outputs[k], axis=1) for k in range(routes)]
        + [
            jnp.sum(input_grad * gain_hidden_cols * hidden_cols, axis=1),
            jnp.sum(input_grad * gain_emb_cols * emb_cols, axis=1),
        ],
        axis=0,
    )
    total = partial + shift(partial, 1) + shift(partial, 2) + shift(partial, 3)
    grad_gate = total[:routes].T
    hidden_dot, emb_dot = total[routes][:, None], total[routes + 1][:, None]
    hidden_cube = hidden_scale * hidden_scale * hidden_scale
    emb_cube = emb_scale * emb_scale * emb_scale
    grad_hidden = gain_hidden_cols * input_grad / hidden_scale - hidden_cols * hidden_dot / (
        width * hidden_cube
    )
    grad_emb = gain_emb_cols * input_grad / emb_scale - emb_cols * emb_dot / (width * emb_cube)
    return moe_out, grad_gate, grad_hidden.astype(BF), grad_emb.astype(BF)


def solution(mesh):
    in_specs = (
        P("ep", None),
        P("ep", "pp"),
        P("ep", None),
        P("ep", None),
        P(),
        P(),
        P("ep", None, "pp"),
        P("ep", None, "pp"),
        P("ep", "pp", None),
        P("ep", "pp"),
    )
    out_specs = (P("ep", "pp"), P("ep", None), P("ep", "pp"), P("ep", "pp"))
    return jax.shard_map(
        per_device, mesh=mesh, in_specs=in_specs, out_specs=out_specs, check_vma=False
    )
```

```python
import jax
import jax.numpy as jnp
from jax import lax
from jax.experimental import pallas as pl
from jax.experimental.pallas import tpu as pltpu
from jax.sharding import PartitionSpec as P

EPS = 1e-06
BF = jnp.bfloat16
F32 = jnp.float32


def dot(left, right, dims):
    return lax.dot_general(left, right, (dims, ((), ())), preferred_element_type=F32)


def shift(value, step):
    ring = lax.axis_size("pp")
    return lax.ppermute(value, "pp", [(i, (i + step) % ring) for i in range(ring)])


def after(value, *others):
    def nothing(*refs):
        pass

    anywhere = pl.BlockSpec(memory_space=pl.ANY)
    return pl.pallas_call(
        nothing,
        out_shape=jax.ShapeDtypeStruct(value.shape, value.dtype),
        in_specs=[anywhere] * (1 + len(others)),
        out_specs=anywhere,
        input_output_aliases={0: 0},
    )(value, *others)


ANYWHERE = pl.BlockSpec(memory_space=pl.ANY)


def params():
    return pltpu.CompilerParams(vmem_limit_bytes=50 * 1024 * 1024)


def ring_gather(own):
    half = own.shape[0] // 2
    below = shift(own, 1)
    above = shift(own, -1)
    return own, above, below, shift(below[:half], 1), shift(above[half:], -1)


def add_halves(up, down, from_below, from_above, *others):
    rows, extended = from_below.shape
    width = up.shape[1]
    skip = extended - width

    def body(up_ref, down_ref, below_ref, above_ref, *refs):
        up_out, down_out = refs[-2:]
        up_out[...] = (up_ref[...].astype(F32) + below_ref[:, skip:].astype(F32)).astype(BF)
        down_out[...] = (down_ref[...].astype(F32) + above_ref[:, skip:].astype(F32)).astype(BF)

    first = pl.BlockSpec((rows // 2, width), lambda i: (i, 0))
    last = pl.BlockSpec((rows // 2, width), lambda i: (2 + i, 0))
    arrived = pl.BlockSpec((rows // 2, extended), lambda i: (i, 0))
    return pl.pallas_call(
        body,
        grid=(2,),
        out_shape=[jax.ShapeDtypeStruct(up.shape, BF)] * 2,
        in_specs=[first, last, arrived, arrived] + [ANYWHERE] * len(others),
        out_specs=[first, last],
        input_output_aliases={0: 0, 1: 1},
        compiler_params=params(),
    )(up, down, from_below, from_above, *others)


def add_and_carry(up, down, from_below, from_above):
    count, width = up.shape
    rows, extended = from_below.shape
    units = (extended - width) // 2
    half = units // 2

    def body(up_ref, down_ref, below_ref, above_ref, up_out, down_out):
        up_out[:, half:] = up_ref[...]
        down_out[:, half:] = down_ref[...]
        for i in range(2):
            here = pl.ds(i * rows, rows)
            up_out[here, :half] = below_ref[:, i * half : (i + 1) * half]
            down_out[here, :half] = above_ref[:, units + i * half : units + (i + 1) * half]
        top, bottom = pl.ds(0, rows), pl.ds(rows, rows)
        below, above = below_ref[:, 2 * units :], above_ref[:, 2 * units :]
        up_out[top, half:] = (up_ref[top, :].astype(F32) + below.astype(F32)).astype(BF)
        down_out[bottom, half:] = (down_ref[bottom, :].astype(F32) + above.astype(F32)).astype(BF)

    return pl.pallas_call(
        body,
        out_shape=[jax.ShapeDtypeStruct((count, half + width), BF)] * 2,
        compiler_params=params(),
    )(up, down, from_below, from_above)


def ring_scatter(from_below, from_above, rest, *others, carry=False):
    up, down, own = rest
    if carry:
        up, down = add_and_carry(up, down, from_below, from_above)
    else:
        up, down = add_halves(up, down, from_below, from_above, *others)
    return (own, shift(up, 1), shift(down, -1)), (up, down)


def sum_beside(left, parts, *others):
    count, quarter = parts[0].shape
    block = count // 2

    def body(left_ref, a_ref, b_ref, c_ref, *refs):
        total = a_ref[...].astype(F32)
        for ref in (b_ref, c_ref):
            total = total + ref[:, ref.shape[1] - quarter :].astype(F32)
        refs[-1][...] = total.astype(BF)

    return pl.pallas_call(
        body,
        grid=(2,),
        out_shape=jax.ShapeDtypeStruct(left.shape, BF),
        in_specs=[ANYWHERE]
        + [pl.BlockSpec((block, p.shape[1]), lambda i: (i, 0)) for p in parts]
        + [ANYWHERE] * len(others),
        out_specs=pl.BlockSpec((block, quarter), lambda i: (i, 1)),
        input_output_aliases={0: 0},
        compiler_params=params(),
    )(left, *parts, *others)


def carried(extended, part, units, *others):
    half = extended.shape[0]

    def body(extended_ref, *refs):
        refs[-1][...] = extended_ref[...]

    return pl.pallas_call(
        body,
        grid=(1,),
        out_shape=jax.ShapeDtypeStruct((half, units), extended.dtype),
        in_specs=[pl.BlockSpec((half, units), lambda i: (0, part))] + [ANYWHERE] * len(others),
        out_specs=pl.BlockSpec((half, units), lambda i: (0, 0)),
        compiler_params=params(),
    )(extended, *others)


def cut_columns(here, array, offset, part, *others):
    rows, width = array.shape
    quarter = width // 4
    steps = 2 if part is None else 1
    first = 0 if part is None else part
    block = rows // 2

    def body(here_ref, array_ref, *refs):
        refs[-1][...] = array_ref[...]

    return pl.pallas_call(
        body,
        grid_spec=pltpu.PrefetchScalarGridSpec(
            num_scalar_prefetch=1,
            grid=(steps,),
            in_specs=[
                pl.BlockSpec((block, quarter), lambda i, here: (i + first, (here[0] + offset) % 4))
            ]
            + [ANYWHERE] * len(others),
            out_specs=pl.BlockSpec((block, quarter), lambda i, here: (i, 0)),
        ),
        out_shape=jax.ShapeDtypeStruct((block * steps, quarter), array.dtype),
        compiler_params=params(),
    )(here, array, *others)


def inner_share(grads, pieces, *others):
    count, quarter = grads.shape
    units = pieces[0].shape[0]
    half = count // 2
    number = len(pieces)

    def body(grads_ref, *refs):
        outs = refs[number + len(others) :]
        shares = [
            dot(grads_ref[...], refs[j][...], ((1,), (1,))).astype(BF) for j in range(number)
        ]
        for i in range(2):

            @pl.when(pl.program_id(0) == i)
            def _():
                for j in range(number):
                    outs[i][:, j * units : (j + 1) * units] = shares[j]

    whole = pl.BlockSpec((units, quarter), lambda i: (0, 0))
    return pl.pallas_call(
        body,
        grid=(2,),
        out_shape=[jax.ShapeDtypeStruct((half, number * units), BF)] * 2,
        in_specs=[pl.BlockSpec((half, quarter), lambda i: (i, 0))]
        + [whole] * number
        + [ANYWHERE] * len(others),
        out_specs=[pl.BlockSpec((half, number * units), lambda i: (0, 0))] * 2,
        compiler_params=params(),
    )(grads, *pieces, *others)


def forward(rows, gate_mat, up_mat, *others):
    count, width = rows.shape
    units = gate_mat.shape[1]
    depth = 1024

    def body(rows_ref, gate_ref, up_ref, *refs):
        gate_out, up_out, act_out = refs[-3:]
        step = pl.program_id(0)

        @pl.when(step == 0)
        def _():
            gate_out[...] = jnp.zeros_like(gate_out)
            up_out[...] = jnp.zeros_like(up_out)

        gate_out[...] += jnp.dot(rows_ref[...], gate_ref[...], preferred_element_type=F32)
        up_out[...] += jnp.dot(rows_ref[...], up_ref[...], preferred_element_type=F32)

        @pl.when(step == pl.num_programs(0) - 1)
        def _():
            gate = gate_out[...]
            act_out[...] = (gate * jax.nn.sigmoid(gate) * up_out[...]).astype(BF)

    whole = pl.BlockSpec((count, units), lambda k: (0, 0))
    weight = pl.BlockSpec((depth, units), lambda k: (k, 0))
    return pl.pallas_call(
        body,
        grid=(width // depth,),
        out_shape=[
            jax.ShapeDtypeStruct((count, units), F32),
            jax.ShapeDtypeStruct((count, units), F32),
            jax.ShapeDtypeStruct((count, units), BF),
        ],
        in_specs=[pl.BlockSpec((count, depth), lambda k: (0, k)), weight, weight]
        + [ANYWHERE] * len(others),
        out_specs=[whole, whole, whole],
        compiler_params=params(),
    )(rows, gate_mat, up_mat, *others)


def backward_far(here, h, gate_pre, up_proj, act, grad_inner, gate_mat, up_mat, *others):
    count, units = gate_pre.shape
    experts, capacity, _ = grad_inner.shape
    quarter = gate_mat.shape[0] // 4
    block = quarter // 2
    half = count // 2

    def body(here_ref, gate_pre_ref, up_ref, act_ref, inner_ref, gate_w, up_w, *refs):
        ggp, gup, low, high = refs[-4:]

        @pl.when(pl.program_id(0) == 0)
        def _():
            inner = inner_ref[...].reshape(count, units)
            gate = gate_pre_ref[...]
            sig = jax.nn.sigmoid(gate)
            ggp[...] = (inner * up_ref[...] * sig * (1.0 + gate * (1.0 - sig))).astype(BF)
            gup[...] = (inner * gate * sig).astype(BF)
            for out in (low, high):
                out[:, :units] = act_ref[:half]
                out[:, units : 2 * units] = act_ref[half:]

        piece = dot(ggp[...], gate_w[...], ((1,), (1,))) + dot(gup[...], up_w[...], ((1,), (1,)))
        for j in range(2):

            @pl.when(pl.program_id(0) == j)
            def _():
                columns = slice(2 * units + j * block, 2 * units + (j + 1) * block)
                low[:, columns] = piece[:half].astype(BF)
                high[:, columns] = piece[half:].astype(BF)

    whole = pl.BlockSpec((count, units), lambda j, here: (0, 0))
    weight = pl.BlockSpec((block, units), lambda j, here: (((here[0] + 2) % 4) * 2 + j, 0))
    out = pl.BlockSpec((half, 2 * units + quarter), lambda j, here: (0, 0))
    return pl.pallas_call(
        body,
        grid_spec=pltpu.PrefetchScalarGridSpec(
            num_scalar_prefetch=1,
            grid=(2,),
            in_specs=[
                whole,
                whole,
                whole,
                pl.BlockSpec((experts, capacity // 2, units), lambda j, here: (0, h, 0)),
                weight,
                weight,
            ]
            + [ANYWHERE] * len(others),
            out_specs=[whole, whole, out, out],
        ),
        out_shape=[
            jax.ShapeDtypeStruct((count, units), BF),
            jax.ShapeDtypeStruct((count, units), BF),
            jax.ShapeDtypeStruct((half, 2 * units + quarter), BF),
            jax.ShapeDtypeStruct((half, 2 * units + quarter), BF),
        ],
        compiler_params=params(),
    )(here, gate_pre, up_proj, act, grad_inner, gate_mat, up_mat, *others)


def backward_rest(here, grad_gate_pre, grad_up, gate_mat, up_mat):
    count, units = grad_up.shape
    quarter = gate_mat.shape[0] // 4
    block = quarter // 2

    def body(here_ref, ggp, gup, gate_w, up_w, *outs):
        step = pl.program_id(0)
        piece = dot(ggp[...], gate_w[...], ((1,), (1,))) + dot(gup[...], up_w[...], ((1,), (1,)))
        piece = piece.astype(BF)
        for i in range(3):

            @pl.when(step // 2 == i)
            def _():
                outs[i][...] = piece

    whole = pl.BlockSpec((count, units), lambda s, here: (0, 0))

    def weight_block(s, here):
        r = jnp.where(s // 2 == 0, 1, jnp.where(s // 2 == 1, 3, 0))
        return (((here[0] + r) % 4) * 2 + s % 2, 0)

    def out_spec(i):
        return pl.BlockSpec((count, block), lambda s, here: (0, jnp.clip(s - 2 * i, 0, 1)))

    weight = pl.BlockSpec((block, units), weight_block)
    return pl.pallas_call(
        body,
        grid_spec=pltpu.PrefetchScalarGridSpec(
            num_scalar_prefetch=1,
            grid=(6,),
            in_specs=[whole, whole, weight, weight],
            out_specs=[out_spec(i) for i in range(3)],
        ),
        out_shape=[jax.ShapeDtypeStruct((count, quarter), BF) for _ in range(3)],
        compiler_params=params(),
    )(here, grad_gate_pre, grad_up, gate_mat, up_mat)


def down_product(acts, downs, *others):
    count, units = acts[0].shape
    quarter = downs[0].shape[1]
    block = 256
    half_units = units // 2

    def body(a0, a1, a3, a2_low, a2_high, *refs):
        down_refs, (out, above, below, far) = refs[: len(downs)], refs[-4:]

        @pl.when(pl.program_id(0) == 0)
        def _():
            for act, rows in ((a2_low, pl.ds(0, count // 2)), (a2_high, pl.ds(count // 2, count // 2))):
                if act.shape[0] == count:
                    far[rows, :half_units] = act[: count // 2]
                    far[rows, half_units:] = act[count // 2 :]
                else:
                    far[rows, :] = act[...]
            for act, full in ((a1, above), (a3, below)):
                full[: count // 2] = act[:, :units]
                full[count // 2 :] = act[:, units : 2 * units]

        total = jnp.dot(a0[...], down_refs[0][...], preferred_element_type=F32)
        total += jnp.dot(above[...], down_refs[1][...], preferred_element_type=F32)
        total += jnp.dot(below[...], down_refs[2][...], preferred_element_type=F32)
        for part in range(2):
            left = far[:, part * half_units : (part + 1) * half_units]
            total += jnp.dot(left, down_refs[3 + part][...], preferred_element_type=F32)
        out[...] = total.astype(BF)

    def held(array):
        return pl.BlockSpec(array.shape, lambda j: (0, 0))

    def streamed(array):
        return pl.BlockSpec((array.shape[0], block), lambda j: (0, j))

    return pl.pallas_call(
        body,
        grid=(quarter // block,),
        out_shape=jax.ShapeDtypeStruct((count, 2 * quarter), BF),
        in_specs=[held(acts[0])]
        + [pl.BlockSpec((count // 2, 2 * units), lambda j: (0, 0))] * 2
        + [
            held(a) if a.shape[1] == units else pl.BlockSpec((count, half_units), lambda j: (0, 0))
            for a in acts[3:]
        ]
        + [streamed(d) for d in downs]
        + [ANYWHERE] * len(others),
        out_specs=pl.BlockSpec((count, block), lambda j: (0, j)),
        scratch_shapes=[pltpu.VMEM((count, units), BF)] * 3,
        compiler_params=params(),
    )(*acts, *downs, *others)


def exchange(value):
    return lax.all_to_all(value, "ep", split_axis=0, concat_axis=0, tiled=True)


def per_device(
    hidden_rows,
    emb_rows,
    expert_ids,
    gate_scores,
    gain_hidden,
    gain_emb,
    gate_weight,
    up_weight,
    down_weight,
    output_grad,
):
    tokens, width = hidden_rows.shape
    quarter = emb_rows.shape[1]
    routes = expert_ids.shape[1]
    experts = lax.axis_size("ep")
    ring = lax.axis_size("pp")
    here = lax.axis_index("pp")
    capacity = 2 * tokens * routes // experts
    part = capacity // 2
    gate_mat, up_mat, down_mat = gate_weight[0], up_weight[0], down_weight[0]
    hidden_units = down_mat.shape[0]

    def columns(array, r):
        return lax.dynamic_slice_in_dim(array, ((here + r) % ring) * quarter, quarter, 1)

    flat_ids = expert_ids.reshape(-1)
    onehot = (flat_ids[:, None] == jnp.arange(experts, dtype=jnp.int32)[None, :]).astype(jnp.int32)
    ranking = jnp.sum(jnp.cumsum(onehot, axis=0) * onehot, axis=1) - 1
    ranking = ranking.reshape(tokens, routes)
    slot_ids = expert_ids * capacity + ranking
    slot_range = jnp.arange(experts * capacity, dtype=jnp.int32)
    selectors = [slot_ids[:, k][:, None] == slot_range[None, :] for k in range(routes)]
    placement = (selectors[0] | selectors[1]).astype(BF)
    slot_score = jnp.sum(
        sum(selectors[k].astype(F32) * gate_scores[:, k : k + 1] for k in range(routes)), axis=0
    )
    part_ids = jnp.where(
        ranking < part,
        expert_ids * part + ranking,
        experts * part + expert_ids * part + ranking - part,
    )
    part_range = jnp.arange(experts * part, dtype=jnp.int32)
    part_selectors = [
        [part_ids[:, k][:, None] == (part_range + h * experts * part)[None, :] for k in range(routes)]
        for h in range(2)
    ]
    part_placement = [(part_selectors[h][0] | part_selectors[h][1]).astype(BF) for h in range(2)]

    emb_own, emb_above, emb_below, emb_low, emb_high = ring_gather(emb_rows)
    emb_pieces = [emb_own, emb_above, jnp.concatenate([emb_low, emb_high], axis=0), emb_below]

    place = here.reshape(1)
    down_low, down_high = (cut_columns(place, down_mat, 2, i) for i in range(2))
    pass_low, pass_high = shift(down_low, 1), shift(down_high, -1)
    far_low, far_high = shift(pass_low, 1), shift(pass_high, -1)

    grad_send = (dot(placement, output_grad, ((0,), (0,))) * slot_score[:, None]).astype(BF)
    grad_send = after(grad_send, down_low, down_high)
    grad_slots = exchange(grad_send.reshape(experts, capacity, quarter))
    grad_slots = grad_slots.reshape(experts * capacity, quarter)

    emb_twice = jnp.concatenate(emb_pieces + emb_pieces, axis=1)
    emb_full = lax.dynamic_slice_in_dim(emb_twice, ((ring - here) % ring) * quarter, width, 1)
    hidden_f = hidden_rows.astype(F32)
    emb_f = emb_full.astype(F32)
    hidden_scale = jnp.sqrt(jnp.mean(hidden_f * hidden_f, axis=1, keepdims=True) + EPS)
    emb_scale = jnp.sqrt(jnp.mean(emb_f * emb_f, axis=1, keepdims=True) + EPS)
    mixed_input = (hidden_f / hidden_scale * gain_hidden + emb_f / emb_scale * gain_emb).astype(BF)
    send_rows = [
        dot(part_placement[h], mixed_input, ((0,), (0,))).astype(BF) for h in range(2)
    ]
    down_up = cut_columns(place, down_mat, 1, None, send_rows[0])
    down_back = cut_columns(place, down_mat, 3, None, send_rows[0])
    down_below, down_above = shift(down_up, 1), shift(down_back, -1)
    down_own = cut_columns(place, down_mat, 0, None, grad_slots)
    far = inner_share(grad_slots, (far_low, far_high))
    own = dot(grad_slots, down_own, ((1,), (1,)))
    send_rows[0] = after(send_rows[0], pass_low, pass_high, down_up, down_back)
    send_rows[1] = after(send_rows[1], *far, own)
    arrived = [
        exchange(send_rows[h].reshape(experts, part, width)).reshape(experts * part, width)
        for h in range(2)
    ]
    downs = (down_own, down_above, down_below, far_low, far_high)
    up = jnp.concatenate(inner_share(grad_slots, (down_above,)), axis=0)
    down = jnp.concatenate(inner_share(grad_slots, (down_below,)), axis=0)
    came = shift(far[0], 1), shift(far[1], -1)
    inner_shares, passed = ring_scatter(*came, (up, down, own))

    for h in range(2):
        gate_pre, up_proj, act = forward(arrived[h], gate_mat, up_mat, *passed)
        if h == 0:
            inner_shares = (after(own, act), *inner_shares[1:])
            grad_inner = sum(share.astype(F32) for share in inner_shares)
            grad_inner = grad_inner.reshape(experts, capacity, hidden_units)
        grad_gate_pre, grad_up, low, high = backward_far(
            place, h, gate_pre, up_proj, act, grad_inner, gate_mat, up_mat
        )
        below, above = shift(low, 1), shift(high, -1)
        rest = backward_rest(place, grad_gate_pre, grad_up, gate_mat, up_mat)
        if h == 0:
            shares, passed = ring_scatter(below, above, rest, carry=True)
            act_low, act_high = shares[1], shares[2]
            first = (act, above, below, act_low, act_high), shares
    first_output = down_product(first[0], downs, low)
    act_low = shift(carried(below, 0, hidden_units, rest[0]), 1)
    act_high = shift(carried(above, 1, hidden_units, rest[0]), -1)
    second, passed = ring_scatter(below, above, rest, act_low, act_high)
    output = down_product((act, above, below, act_low, act_high), downs, *passed)
    returned = [
        exchange(both.reshape(experts, part, 2 * quarter))
        for both in (
            sum_beside(first_output, first[1], below, above, rest[0]),
            sum_beside(output, second),
        )
    ]
    returned = [both.reshape(experts * part, 2 * quarter) for both in returned]
    back = [both[:, :quarter] for both in returned]
    grads_back = [both[:, quarter:] for both in returned]

    route_outputs = [
        sum(dot(part_selectors[h][k].astype(BF), back[h], ((1,), (0,))) for h in range(2))
        for k in range(routes)
    ]
    moe_out = sum(gate_scores[:, k : k + 1] * route_outputs[k] for k in range(routes)).astype(BF)
    input_grad = sum(dot(part_placement[h], grads_back[h], ((1,), (0,))) for h in range(2))

    grad_f = output_grad.astype(F32)
    hidden_cols = columns(hidden_rows, 0).astype(F32)
    emb_cols = emb_rows.astype(F32)
    gain_hidden_cols = lax.dynamic_slice_in_dim(gain_hidden, here * quarter, quarter, 0)
    gain_emb_cols = lax.dynamic_slice_in_dim(gain_emb, here * quarter, quarter, 0)
    partial = jnp.stack(
        [jnp.sum(grad_f * route_outputs[k], axis=1) for k in range(routes)]
        + [
            jnp.sum(input_grad * gain_hidden_cols * hidden_cols, axis=1),
            jnp.sum(input_grad * gain_emb_cols * emb_cols, axis=1),
        ],
        axis=0,
    )
    total = partial + shift(partial, 1) + shift(partial, 2) + shift(partial, 3)
    grad_gate = total[:routes].T
    hidden_dot, emb_dot = total[routes][:, None], total[routes + 1][:, None]
    hidden_cube = hidden_scale * hidden_scale * hidden_scale
    emb_cube = emb_scale * emb_scale * emb_scale
    grad_hidden = gain_hidden_cols * input_grad / hidden_scale - hidden_cols * hidden_dot / (
        width * hidden_cube
    )
    grad_emb = gain_emb_cols * input_grad / emb_scale - emb_cols * emb_dot / (width * emb_cube)
    return moe_out, grad_gate, grad_hidden.astype(BF), grad_emb.astype(BF)


def solution(mesh):
    in_specs = (
        P("ep", None),
        P("ep", "pp"),
        P("ep", None),
        P("ep", None),
        P(),
        P(),
        P("ep", None, "pp"),
        P("ep", None, "pp"),
        P("ep", "pp", None),
        P("ep", "pp"),
    )
    out_specs = (P("ep", "pp"), P("ep", None), P("ep", "pp"), P("ep", "pp"))
    return jax.shard_map(
        per_device, mesh=mesh, in_specs=in_specs, out_specs=out_specs, check_vma=False
    )
```

```python
import jax
import jax.numpy as jnp
from jax import lax
from jax.experimental import pallas as pl
from jax.experimental.pallas import tpu as pltpu
from jax.sharding import PartitionSpec as P

EPS = 1e-06
BF = jnp.bfloat16
F32 = jnp.float32


def dot(left, right, dims):
    return lax.dot_general(left, right, (dims, ((), ())), preferred_element_type=F32)


def shift(value, step):
    ring = lax.axis_size("pp")
    return lax.ppermute(value, "pp", [(i, (i + step) % ring) for i in range(ring)])


def after(value, *others):
    def nothing(*refs):
        pass

    anywhere = pl.BlockSpec(memory_space=pl.ANY)
    return pl.pallas_call(
        nothing,
        out_shape=jax.ShapeDtypeStruct(value.shape, value.dtype),
        in_specs=[anywhere] * (1 + len(others)),
        out_specs=anywhere,
        input_output_aliases={0: 0},
    )(value, *others)


ANYWHERE = pl.BlockSpec(memory_space=pl.ANY)


def params():
    return pltpu.CompilerParams(vmem_limit_bytes=50 * 1024 * 1024)


def ring_gather(own):
    half = own.shape[0] // 2
    below = shift(own, 1)
    above = shift(own, -1)
    return own, above, below, shift(below[:half], 1), shift(above[half:], -1)


def add_halves(up, down, from_below, from_above, *others):
    rows, extended = from_below.shape
    width = up.shape[1]
    skip = extended - width

    def body(up_ref, down_ref, below_ref, above_ref, *refs):
        up_out, down_out = refs[-2:]
        up_out[...] = (up_ref[...].astype(F32) + below_ref[:, skip:].astype(F32)).astype(BF)
        down_out[...] = (down_ref[...].astype(F32) + above_ref[:, skip:].astype(F32)).astype(BF)

    first = pl.BlockSpec((rows // 2, width), lambda i: (i, 0))
    last = pl.BlockSpec((rows // 2, width), lambda i: (2 + i, 0))
    arrived = pl.BlockSpec((rows // 2, extended), lambda i: (i, 0))
    return pl.pallas_call(
        body,
        grid=(2,),
        out_shape=[jax.ShapeDtypeStruct(up.shape, BF)] * 2,
        in_specs=[first, last, arrived, arrived] + [ANYWHERE] * len(others),
        out_specs=[first, last],
        input_output_aliases={0: 0, 1: 1},
        compiler_params=params(),
    )(up, down, from_below, from_above, *others)


def add_and_carry(up, down, from_below, from_above):
    count, width = up.shape
    rows, extended = from_below.shape
    units = (extended - width) // 2
    half = units // 2

    def body(up_ref, down_ref, below_ref, above_ref, up_out, down_out):
        up_out[:, half:] = up_ref[...]
        down_out[:, half:] = down_ref[...]
        for i in range(2):
            here = pl.ds(i * rows, rows)
            up_out[here, :half] = below_ref[:, i * half : (i + 1) * half]
            down_out[here, :half] = above_ref[:, units + i * half : units + (i + 1) * half]
        top, bottom = pl.ds(0, rows), pl.ds(rows, rows)
        below, above = below_ref[:, 2 * units :], above_ref[:, 2 * units :]
        up_out[top, half:] = (up_ref[top, :].astype(F32) + below.astype(F32)).astype(BF)
        down_out[bottom, half:] = (down_ref[bottom, :].astype(F32) + above.astype(F32)).astype(BF)

    return pl.pallas_call(
        body,
        out_shape=[jax.ShapeDtypeStruct((count, half + width), BF)] * 2,
        compiler_params=params(),
    )(up, down, from_below, from_above)


def ring_scatter(from_below, from_above, rest, *others, carry=False):
    up, down, own = rest
    if carry:
        up, down = add_and_carry(up, down, from_below, from_above)
    else:
        up, down = add_halves(up, down, from_below, from_above, *others)
    return (own, shift(up, 1), shift(down, -1)), (up, down)


def sum_beside(left, parts, *others):
    count, quarter = parts[0].shape
    block = count // 2

    def body(left_ref, a_ref, b_ref, c_ref, *refs):
        total = a_ref[...].astype(F32)
        for ref in (b_ref, c_ref):
            total = total + ref[:, ref.shape[1] - quarter :].astype(F32)
        refs[-1][...] = total.astype(BF)

    return pl.pallas_call(
        body,
        grid=(2,),
        out_shape=jax.ShapeDtypeStruct(left.shape, BF),
        in_specs=[ANYWHERE]
        + [pl.BlockSpec((block, p.shape[1]), lambda i: (i, 0)) for p in parts]
        + [ANYWHERE] * len(others),
        out_specs=pl.BlockSpec((block, quarter), lambda i: (i, 1)),
        input_output_aliases={0: 0},
        compiler_params=params(),
    )(left, *parts, *others)


def carried(extended, part, units, *others):
    half = extended.shape[0]

    def body(extended_ref, *refs):
        refs[-1][...] = extended_ref[...]

    return pl.pallas_call(
        body,
        grid=(1,),
        out_shape=jax.ShapeDtypeStruct((half, units), extended.dtype),
        in_specs=[pl.BlockSpec((half, units), lambda i: (0, part))] + [ANYWHERE] * len(others),
        out_specs=pl.BlockSpec((half, units), lambda i: (0, 0)),
        compiler_params=params(),
    )(extended, *others)


def cut_columns(here, array, offset, part, *others):
    rows, width = array.shape
    quarter = width // 4
    steps = 2 if part is None else 1
    first = 0 if part is None else part
    block = rows // 2

    def body(here_ref, array_ref, *refs):
        refs[-1][...] = array_ref[...]

    return pl.pallas_call(
        body,
        grid_spec=pltpu.PrefetchScalarGridSpec(
            num_scalar_prefetch=1,
            grid=(steps,),
            in_specs=[
                pl.BlockSpec((block, quarter), lambda i, here: (i + first, (here[0] + offset) % 4))
            ]
            + [ANYWHERE] * len(others),
            out_specs=pl.BlockSpec((block, quarter), lambda i, here: (i, 0)),
        ),
        out_shape=jax.ShapeDtypeStruct((block * steps, quarter), array.dtype),
        compiler_params=params(),
    )(here, array, *others)


def inner_share(grads, pieces, *others):
    count, quarter = grads.shape
    units = pieces[0].shape[0]
    half = count // 2
    number = len(pieces)

    def body(grads_ref, *refs):
        outs = refs[number + len(others) :]
        shares = [
            dot(grads_ref[...], refs[j][...], ((1,), (1,))).astype(BF) for j in range(number)
        ]
        for i in range(2):

            @pl.when(pl.program_id(0) == i)
            def _():
                for j in range(number):
                    outs[i][:, j * units : (j + 1) * units] = shares[j]

    whole = pl.BlockSpec((units, quarter), lambda i: (0, 0))
    return pl.pallas_call(
        body,
        grid=(2,),
        out_shape=[jax.ShapeDtypeStruct((half, number * units), BF)] * 2,
        in_specs=[pl.BlockSpec((half, quarter), lambda i: (i, 0))]
        + [whole] * number
        + [ANYWHERE] * len(others),
        out_specs=[pl.BlockSpec((half, number * units), lambda i: (0, 0))] * 2,
        compiler_params=params(),
    )(grads, *pieces, *others)


def forward(rows, gate_mat, up_mat, *others):
    count, width = rows.shape
    units = gate_mat.shape[1]
    depth = 1024

    def body(rows_ref, gate_ref, up_ref, *refs):
        gate_out, up_out, act_out = refs[-3:]
        step = pl.program_id(0)

        @pl.when(step == 0)
        def _():
            gate_out[...] = jnp.zeros_like(gate_out)
            up_out[...] = jnp.zeros_like(up_out)

        gate_out[...] += jnp.dot(rows_ref[...], gate_ref[...], preferred_element_type=F32)
        up_out[...] += jnp.dot(rows_ref[...], up_ref[...], preferred_element_type=F32)

        @pl.when(step == pl.num_programs(0) - 1)
        def _():
            gate = gate_out[...]
            act_out[...] = (gate * jax.nn.sigmoid(gate) * up_out[...]).astype(BF)

    whole = pl.BlockSpec((count, units), lambda k: (0, 0))
    weight = pl.BlockSpec((depth, units), lambda k: (k, 0))
    return pl.pallas_call(
        body,
        grid=(width // depth,),
        out_shape=[
            jax.ShapeDtypeStruct((count, units), F32),
            jax.ShapeDtypeStruct((count, units), F32),
            jax.ShapeDtypeStruct((count, units), BF),
        ],
        in_specs=[pl.BlockSpec((count, depth), lambda k: (0, k)), weight, weight]
        + [ANYWHERE] * len(others),
        out_specs=[whole, whole, whole],
        compiler_params=params(),
    )(rows, gate_mat, up_mat, *others)


def backward_far(here, h, gate_pre, up_proj, act, grad_inner, gate_mat, up_mat, *others):
    count, units = gate_pre.shape
    experts, capacity, _ = grad_inner.shape
    quarter = gate_mat.shape[0] // 4
    block = quarter // 2
    half = count // 2

    def body(here_ref, gate_pre_ref, up_ref, act_ref, inner_ref, gate_w, up_w, *refs):
        ggp, gup, low, high = refs[-4:]

        @pl.when(pl.program_id(0) == 0)
        def _():
            inner = inner_ref[...].reshape(count, units)
            gate = gate_pre_ref[...]
            sig = jax.nn.sigmoid(gate)
            ggp[...] = (inner * up_ref[...] * sig * (1.0 + gate * (1.0 - sig))).astype(BF)
            gup[...] = (inner * gate * sig).astype(BF)
            for out in (low, high):
                out[:, :units] = act_ref[:half]
                out[:, units : 2 * units] = act_ref[half:]

        piece = dot(ggp[...], gate_w[...], ((1,), (1,))) + dot(gup[...], up_w[...], ((1,), (1,)))
        for j in range(2):

            @pl.when(pl.program_id(0) == j)
            def _():
                columns = slice(2 * units + j * block, 2 * units + (j + 1) * block)
                low[:, columns] = piece[:half].astype(BF)
                high[:, columns] = piece[half:].astype(BF)

    whole = pl.BlockSpec((count, units), lambda j, here: (0, 0))
    weight = pl.BlockSpec((block, units), lambda j, here: (((here[0] + 2) % 4) * 2 + j, 0))
    out = pl.BlockSpec((half, 2 * units + quarter), lambda j, here: (0, 0))
    return pl.pallas_call(
        body,
        grid_spec=pltpu.PrefetchScalarGridSpec(
            num_scalar_prefetch=1,
            grid=(2,),
            in_specs=[
                whole,
                whole,
                whole,
                pl.BlockSpec((experts, capacity // 2, units), lambda j, here: (0, h, 0)),
                weight,
                weight,
            ]
            + [ANYWHERE] * len(others),
            out_specs=[whole, whole, out, out],
        ),
        out_shape=[
            jax.ShapeDtypeStruct((count, units), BF),
            jax.ShapeDtypeStruct((count, units), BF),
            jax.ShapeDtypeStruct((half, 2 * units + quarter), BF),
            jax.ShapeDtypeStruct((half, 2 * units + quarter), BF),
        ],
        compiler_params=params(),
    )(here, gate_pre, up_proj, act, grad_inner, gate_mat, up_mat, *others)


def backward_rest(here, grad_gate_pre, grad_up, gate_mat, up_mat):
    count, units = grad_up.shape
    quarter = gate_mat.shape[0] // 4
    block = quarter // 2

    def body(here_ref, ggp, gup, gate_w, up_w, *outs):
        step = pl.program_id(0)
        piece = dot(ggp[...], gate_w[...], ((1,), (1,))) + dot(gup[...], up_w[...], ((1,), (1,)))
        piece = piece.astype(BF)
        for i in range(3):

            @pl.when(step // 2 == i)
            def _():
                outs[i][...] = piece

    whole = pl.BlockSpec((count, units), lambda s, here: (0, 0))

    def weight_block(s, here):
        r = jnp.where(s // 2 == 0, 1, jnp.where(s // 2 == 1, 3, 0))
        return (((here[0] + r) % 4) * 2 + s % 2, 0)

    def out_spec(i):
        return pl.BlockSpec((count, block), lambda s, here: (0, jnp.clip(s - 2 * i, 0, 1)))

    weight = pl.BlockSpec((block, units), weight_block)
    return pl.pallas_call(
        body,
        grid_spec=pltpu.PrefetchScalarGridSpec(
            num_scalar_prefetch=1,
            grid=(6,),
            in_specs=[whole, whole, weight, weight],
            out_specs=[out_spec(i) for i in range(3)],
        ),
        out_shape=[jax.ShapeDtypeStruct((count, quarter), BF) for _ in range(3)],
        compiler_params=params(),
    )(here, grad_gate_pre, grad_up, gate_mat, up_mat)


def down_product(acts, downs, *others):
    count, units = acts[0].shape
    quarter = downs[0].shape[1]
    block = 256
    half_units = units // 2

    def body(a0, a1, a3, a2_low, a2_high, *refs):
        down_refs, (out, above, below, far) = refs[: len(downs)], refs[-4:]

        @pl.when(pl.program_id(0) == 0)
        def _():
            for act, rows in ((a2_low, pl.ds(0, count // 2)), (a2_high, pl.ds(count // 2, count // 2))):
                if act.shape[0] == count:
                    far[rows, :half_units] = act[: count // 2]
                    far[rows, half_units:] = act[count // 2 :]
                else:
                    far[rows, :] = act[...]
            for act, full in ((a1, above), (a3, below)):
                full[: count // 2] = act[:, :units]
                full[count // 2 :] = act[:, units : 2 * units]

        total = jnp.dot(a0[...], down_refs[0][...], preferred_element_type=F32)
        total += jnp.dot(above[...], down_refs[1][...], preferred_element_type=F32)
        total += jnp.dot(below[...], down_refs[2][...], preferred_element_type=F32)
        for part in range(2):
            left = far[:, part * half_units : (part + 1) * half_units]
            total += jnp.dot(left, down_refs[3 + part][...], preferred_element_type=F32)
        out[...] = total.astype(BF)

    def held(array):
        return pl.BlockSpec(array.shape, lambda j: (0, 0))

    def streamed(array):
        return pl.BlockSpec((array.shape[0], block), lambda j: (0, j))

    return pl.pallas_call(
        body,
        grid=(quarter // block,),
        out_shape=jax.ShapeDtypeStruct((count, 2 * quarter), BF),
        in_specs=[held(acts[0])]
        + [pl.BlockSpec((count // 2, 2 * units), lambda j: (0, 0))] * 2
        + [
            held(a) if a.shape[1] == units else pl.BlockSpec((count, half_units), lambda j: (0, 0))
            for a in acts[3:]
        ]
        + [streamed(d) for d in downs]
        + [ANYWHERE] * len(others),
        out_specs=pl.BlockSpec((count, block), lambda j: (0, j)),
        scratch_shapes=[pltpu.VMEM((count, units), BF)] * 3,
        compiler_params=params(),
    )(*acts, *downs, *others)


def token_sums(returned, bases, selectors, scores, grads, hidden, emb, gain_hidden, gain_emb):
    tokens, quarter = grads.shape
    rows = returned.shape[0]
    block = quarter // 2

    def body(y, z, b0, b1, b2, s0, s1, score, grad, hid, em, gh, ge, moe, ig, sums):
        first = b0[...] + jnp.dot(s0[...], y[...], preferred_element_type=F32)
        second = b1[...] + jnp.dot(s1[...], y[...], preferred_element_type=F32)
        both = s0[...] + s1[...]
        inputs = b2[...] + jnp.dot(both, z[...], preferred_element_type=F32)
        moe[...] = (score[:, 0:1] * first + score[:, 1:2] * second).astype(BF)
        ig[...] = inputs
        grad_f = grad[...].astype(F32)
        terms = (
            grad_f * first,
            grad_f * second,
            inputs * gh[...] * hid[...].astype(F32),
            inputs * ge[...] * em[...].astype(F32),
        )
        lane = lax.broadcasted_iota(jnp.int32, (tokens, 128), 1)
        total = jnp.zeros((tokens, 128), F32)
        for k, term in enumerate(terms):
            total = jnp.where(lane == k, jnp.sum(term, axis=1, keepdims=True), total)

        @pl.when(pl.program_id(0) == 0)
        def _():
            sums[...] = total

        @pl.when(pl.program_id(0) == 1)
        def _():
            sums[...] += total

    columns = pl.BlockSpec((tokens, block), lambda j: (0, j))
    gain = pl.BlockSpec((1, block), lambda j: (0, j))
    held = pl.BlockSpec((tokens, rows), lambda j: (0, 0))
    return pl.pallas_call(
        body,
        grid=(2,),
        out_shape=[
            jax.ShapeDtypeStruct((tokens, quarter), BF),
            jax.ShapeDtypeStruct((tokens, quarter), F32),
            jax.ShapeDtypeStruct((tokens, 128), F32),
        ],
        in_specs=[
            pl.BlockSpec((rows, block), lambda j: (0, j)),
            pl.BlockSpec((rows, block), lambda j: (0, 2 + j)),
            columns,
            columns,
            columns,
            held,
            held,
            pl.BlockSpec(scores.shape, lambda j: (0, 0)),
            columns,
            columns,
            columns,
            gain,
            gain,
        ],
        out_specs=[columns, columns, pl.BlockSpec((tokens, 128), lambda j: (0, 0))],
        compiler_params=params(),
    )(
        returned, returned, *bases, *selectors, scores, grads, hidden, emb, gain_hidden, gain_emb
    )


def exchange(value):
    return lax.all_to_all(value, "ep", split_axis=0, concat_axis=0, tiled=True)


def per_device(
    hidden_rows,
    emb_rows,
    expert_ids,
    gate_scores,
    gain_hidden,
    gain_emb,
    gate_weight,
    up_weight,
    down_weight,
    output_grad,
):
    tokens, width = hidden_rows.shape
    quarter = emb_rows.shape[1]
    routes = expert_ids.shape[1]
    experts = lax.axis_size("ep")
    ring = lax.axis_size("pp")
    here = lax.axis_index("pp")
    capacity = 2 * tokens * routes // experts
    part = capacity // 2
    gate_mat, up_mat, down_mat = gate_weight[0], up_weight[0], down_weight[0]
    hidden_units = down_mat.shape[0]

    def columns(array, r):
        return lax.dynamic_slice_in_dim(array, ((here + r) % ring) * quarter, quarter, 1)

    flat_ids = expert_ids.reshape(-1)
    onehot = (flat_ids[:, None] == jnp.arange(experts, dtype=jnp.int32)[None, :]).astype(jnp.int32)
    ranking = jnp.sum(jnp.cumsum(onehot, axis=0) * onehot, axis=1) - 1
    ranking = ranking.reshape(tokens, routes)
    slot_ids = expert_ids * capacity + ranking
    slot_range = jnp.arange(experts * capacity, dtype=jnp.int32)
    selectors = [slot_ids[:, k][:, None] == slot_range[None, :] for k in range(routes)]
    placement = (selectors[0] | selectors[1]).astype(BF)
    slot_score = jnp.sum(
        sum(selectors[k].astype(F32) * gate_scores[:, k : k + 1] for k in range(routes)), axis=0
    )
    part_ids = jnp.where(
        ranking < part,
        expert_ids * part + ranking,
        experts * part + expert_ids * part + ranking - part,
    )
    part_range = jnp.arange(experts * part, dtype=jnp.int32)
    part_selectors = [
        [part_ids[:, k][:, None] == (part_range + h * experts * part)[None, :] for k in range(routes)]
        for h in range(2)
    ]
    part_placement = [(part_selectors[h][0] | part_selectors[h][1]).astype(BF) for h in range(2)]

    emb_own, emb_above, emb_below, emb_low, emb_high = ring_gather(emb_rows)
    emb_pieces = [emb_own, emb_above, jnp.concatenate([emb_low, emb_high], axis=0), emb_below]

    place = here.reshape(1)
    down_low, down_high = (cut_columns(place, down_mat, 2, i) for i in range(2))
    pass_low, pass_high = shift(down_low, 1), shift(down_high, -1)
    far_low, far_high = shift(pass_low, 1), shift(pass_high, -1)

    grad_send = (dot(placement, output_grad, ((0,), (0,))) * slot_score[:, None]).astype(BF)
    grad_send = after(grad_send, down_low, down_high)
    grad_slots = exchange(grad_send.reshape(experts, capacity, quarter))
    grad_slots = grad_slots.reshape(experts * capacity, quarter)

    emb_twice = jnp.concatenate(emb_pieces + emb_pieces, axis=1)
    emb_full = lax.dynamic_slice_in_dim(emb_twice, ((ring - here) % ring) * quarter, width, 1)
    hidden_f = hidden_rows.astype(F32)
    emb_f = emb_full.astype(F32)
    hidden_scale = jnp.sqrt(jnp.mean(hidden_f * hidden_f, axis=1, keepdims=True) + EPS)
    emb_scale = jnp.sqrt(jnp.mean(emb_f * emb_f, axis=1, keepdims=True) + EPS)
    mixed_input = (hidden_f / hidden_scale * gain_hidden + emb_f / emb_scale * gain_emb).astype(BF)
    send_rows = [
        dot(part_placement[h], mixed_input, ((0,), (0,))).astype(BF) for h in range(2)
    ]
    down_up = cut_columns(place, down_mat, 1, None, send_rows[0])
    down_back = cut_columns(place, down_mat, 3, None, send_rows[0])
    down_below, down_above = shift(down_up, 1), shift(down_back, -1)
    down_own = cut_columns(place, down_mat, 0, None, grad_slots)
    far = inner_share(grad_slots, (far_low, far_high))
    own = dot(grad_slots, down_own, ((1,), (1,)))
    send_rows[0] = after(send_rows[0], pass_low, pass_high, down_up, down_back)
    send_rows[1] = after(send_rows[1], *far, own)
    arrived = [
        exchange(send_rows[h].reshape(experts, part, width)).reshape(experts * part, width)
        for h in range(2)
    ]
    downs = (down_own, down_above, down_below, far_low, far_high)
    up = jnp.concatenate(inner_share(grad_slots, (down_above,)), axis=0)
    down = jnp.concatenate(inner_share(grad_slots, (down_below,)), axis=0)
    came = shift(far[0], 1), shift(far[1], -1)
    inner_shares, passed = ring_scatter(*came, (up, down, own))

    for h in range(2):
        gate_pre, up_proj, act = forward(arrived[h], gate_mat, up_mat, *passed)
        if h == 0:
            inner_shares = (after(own, act), *inner_shares[1:])
            grad_inner = sum(share.astype(F32) for share in inner_shares)
            grad_inner = grad_inner.reshape(experts, capacity, hidden_units)
        grad_gate_pre, grad_up, low, high = backward_far(
            place, h, gate_pre, up_proj, act, grad_inner, gate_mat, up_mat
        )
        below, above = shift(low, 1), shift(high, -1)
        rest = backward_rest(place, grad_gate_pre, grad_up, gate_mat, up_mat)
        if h == 0:
            shares, passed = ring_scatter(below, above, rest, carry=True)
            act_low, act_high = shares[1], shares[2]
            first = (act, above, below, act_low, act_high), shares
    first_output = down_product(first[0], downs, low)
    act_low = shift(carried(below, 0, hidden_units, rest[0]), 1)
    act_high = shift(carried(above, 1, hidden_units, rest[0]), -1)
    second, passed = ring_scatter(below, above, rest, act_low, act_high)
    output = down_product((act, above, below, act_low, act_high), downs, *passed)
    returned = [
        exchange(both.reshape(experts, part, 2 * quarter))
        for both in (
            sum_beside(first_output, first[1], below, above, rest[0]),
            sum_beside(output, second),
        )
    ]
    returned = [both.reshape(experts * part, 2 * quarter) for both in returned]
    outputs_back, grads_back = returned[0][:, :quarter], returned[0][:, quarter:]
    bases = [
        dot(part_selectors[0][k].astype(BF), outputs_back, ((1,), (0,))) for k in range(routes)
    ]
    bases.append(dot(part_placement[0], grads_back, ((1,), (0,))))
    hidden_cols = columns(hidden_rows, 0)
    gain_hidden_cols = lax.dynamic_slice_in_dim(gain_hidden, here * quarter, quarter, 0)[None]
    gain_emb_cols = lax.dynamic_slice_in_dim(gain_emb, here * quarter, quarter, 0)[None]
    moe_out, input_grad, partial = token_sums(
        returned[1],
        bases,
        [part_selectors[1][k].astype(BF) for k in range(routes)],
        gate_scores,
        output_grad,
        hidden_cols,
        emb_rows,
        gain_hidden_cols,
        gain_emb_cols,
    )
    total = partial + shift(partial, 1) + shift(partial, 2) + shift(partial, 3)
    grad_gate = total[:, :routes]
    hidden_dot, emb_dot = total[:, routes : routes + 1], total[:, routes + 1 : routes + 2]
    hidden_cols, emb_cols = hidden_cols.astype(F32), emb_rows.astype(F32)
    hidden_cube = hidden_scale * hidden_scale * hidden_scale
    emb_cube = emb_scale * emb_scale * emb_scale
    grad_hidden = gain_hidden_cols * input_grad / hidden_scale - hidden_cols * hidden_dot / (
        width * hidden_cube
    )
    grad_emb = gain_emb_cols * input_grad / emb_scale - emb_cols * emb_dot / (width * emb_cube)
    return moe_out, grad_gate, grad_hidden.astype(BF), grad_emb.astype(BF)


def solution(mesh):
    in_specs = (
        P("ep", None),
        P("ep", "pp"),
        P("ep", None),
        P("ep", None),
        P(),
        P(),
        P("ep", None, "pp"),
        P("ep", None, "pp"),
        P("ep", "pp", None),
        P("ep", "pp"),
    )
    out_specs = (P("ep", "pp"), P("ep", None), P("ep", "pp"), P("ep", "pp"))
    return jax.shard_map(
        per_device, mesh=mesh, in_specs=in_specs, out_specs=out_specs, check_vma=False
    )
```

```python
import jax
import jax.numpy as jnp
from jax import lax
from jax.experimental import pallas as pl
from jax.experimental.pallas import tpu as pltpu
from jax.sharding import PartitionSpec as P

EPS = 1e-06
BF = jnp.bfloat16
F32 = jnp.float32


def dot(left, right, dims):
    return lax.dot_general(left, right, (dims, ((), ())), preferred_element_type=F32)


def shift(value, step):
    ring = lax.axis_size("pp")
    return lax.ppermute(value, "pp", [(i, (i + step) % ring) for i in range(ring)])


def after(value, *others):
    def nothing(*refs):
        pass

    anywhere = pl.BlockSpec(memory_space=pl.ANY)
    return pl.pallas_call(
        nothing,
        out_shape=jax.ShapeDtypeStruct(value.shape, value.dtype),
        in_specs=[anywhere] * (1 + len(others)),
        out_specs=anywhere,
        input_output_aliases={0: 0},
    )(value, *others)


ANYWHERE = pl.BlockSpec(memory_space=pl.ANY)


def params():
    return pltpu.CompilerParams(vmem_limit_bytes=50 * 1024 * 1024)


def ring_gather(own):
    half = own.shape[0] // 2
    below = shift(own, 1)
    above = shift(own, -1)
    return own, above, below, shift(below[:half], 1), shift(above[half:], -1)


def add_halves(up, down, from_below, from_above, *others):
    rows, extended = from_below.shape
    width = up.shape[1]
    skip = extended - width

    def body(up_ref, down_ref, below_ref, above_ref, *refs):
        up_out, down_out = refs[-2:]
        up_out[...] = (up_ref[...].astype(F32) + below_ref[:, skip:].astype(F32)).astype(BF)
        down_out[...] = (down_ref[...].astype(F32) + above_ref[:, skip:].astype(F32)).astype(BF)

    first = pl.BlockSpec((rows // 2, width), lambda i: (i, 0))
    last = pl.BlockSpec((rows // 2, width), lambda i: (2 + i, 0))
    arrived = pl.BlockSpec((rows // 2, extended), lambda i: (i, 0))
    return pl.pallas_call(
        body,
        grid=(2,),
        out_shape=[jax.ShapeDtypeStruct(up.shape, BF)] * 2,
        in_specs=[first, last, arrived, arrived] + [ANYWHERE] * len(others),
        out_specs=[first, last],
        input_output_aliases={0: 0, 1: 1},
        compiler_params=params(),
    )(up, down, from_below, from_above, *others)


def add_and_carry(up, down, from_below, from_above):
    count, width = up.shape
    rows, extended = from_below.shape
    units = (extended - width) // 2
    half = units // 2

    def body(up_ref, down_ref, below_ref, above_ref, up_out, down_out):
        up_out[:, half:] = up_ref[...]
        down_out[:, half:] = down_ref[...]
        for i in range(2):
            here = pl.ds(i * rows, rows)
            up_out[here, :half] = below_ref[:, i * half : (i + 1) * half]
            down_out[here, :half] = above_ref[:, units + i * half : units + (i + 1) * half]
        top, bottom = pl.ds(0, rows), pl.ds(rows, rows)
        below, above = below_ref[:, 2 * units :], above_ref[:, 2 * units :]
        up_out[top, half:] = (up_ref[top, :].astype(F32) + below.astype(F32)).astype(BF)
        down_out[bottom, half:] = (down_ref[bottom, :].astype(F32) + above.astype(F32)).astype(BF)

    return pl.pallas_call(
        body,
        out_shape=[jax.ShapeDtypeStruct((count, half + width), BF)] * 2,
        compiler_params=params(),
    )(up, down, from_below, from_above)


def ring_scatter(from_below, from_above, rest, *others, carry=False):
    up, down, own = rest
    if carry:
        up, down = add_and_carry(up, down, from_below, from_above)
    else:
        up, down = add_halves(up, down, from_below, from_above, *others)
    return (own, shift(up, 1), shift(down, -1)), (up, down)


def sum_beside(left, parts, *others):
    count, quarter = parts[0].shape
    block = count // 2

    def body(left_ref, a_ref, b_ref, c_ref, *refs):
        total = a_ref[...].astype(F32)
        for ref in (b_ref, c_ref):
            total = total + ref[:, ref.shape[1] - quarter :].astype(F32)
        refs[-1][...] = total.astype(BF)

    return pl.pallas_call(
        body,
        grid=(2,),
        out_shape=jax.ShapeDtypeStruct(left.shape, BF),
        in_specs=[ANYWHERE]
        + [pl.BlockSpec((block, p.shape[1]), lambda i: (i, 0)) for p in parts]
        + [ANYWHERE] * len(others),
        out_specs=pl.BlockSpec((block, quarter), lambda i: (i, 1)),
        input_output_aliases={0: 0},
        compiler_params=params(),
    )(left, *parts, *others)


def carried(extended, part, units, *others):
    half = extended.shape[0]

    def body(extended_ref, *refs):
        refs[-1][...] = extended_ref[...]

    return pl.pallas_call(
        body,
        grid=(1,),
        out_shape=jax.ShapeDtypeStruct((half, units), extended.dtype),
        in_specs=[pl.BlockSpec((half, units), lambda i: (0, part))] + [ANYWHERE] * len(others),
        out_specs=pl.BlockSpec((half, units), lambda i: (0, 0)),
        compiler_params=params(),
    )(extended, *others)


def cut_columns(here, array, offset, first, rows, *others):
    quarter = array.shape[1] // 4
    block = 128

    def body(here_ref, array_ref, *refs):
        refs[-1][...] = array_ref[...]

    return pl.pallas_call(
        body,
        grid_spec=pltpu.PrefetchScalarGridSpec(
            num_scalar_prefetch=1,
            grid=(rows // block,),
            in_specs=[
                pl.BlockSpec(
                    (block, quarter), lambda i, here: (i + first // block, (here[0] + offset) % 4)
                )
            ]
            + [ANYWHERE] * len(others),
            out_specs=pl.BlockSpec((block, quarter), lambda i, here: (i, 0)),
        ),
        out_shape=jax.ShapeDtypeStruct((rows, quarter), array.dtype),
        compiler_params=params(),
    )(here, array, *others)


def inner_share(grads, pieces, *others):
    count, quarter = grads.shape
    units = pieces[0].shape[0]
    half = count // 2
    number = len(pieces)

    def body(grads_ref, *refs):
        outs = refs[number + len(others) :]
        shares = [
            dot(grads_ref[...], refs[j][...], ((1,), (1,))).astype(BF) for j in range(number)
        ]
        for i in range(2):

            @pl.when(pl.program_id(0) == i)
            def _():
                for j in range(number):
                    outs[i][:, j * units : (j + 1) * units] = shares[j]

    whole = pl.BlockSpec((units, quarter), lambda i: (0, 0))
    return pl.pallas_call(
        body,
        grid=(2,),
        out_shape=[jax.ShapeDtypeStruct((half, number * units), BF)] * 2,
        in_specs=[pl.BlockSpec((half, quarter), lambda i: (i, 0))]
        + [whole] * number
        + [ANYWHERE] * len(others),
        out_specs=[pl.BlockSpec((half, number * units), lambda i: (0, 0))] * 2,
        compiler_params=params(),
    )(grads, *pieces, *others)


def forward(rows, gate_mat, up_mat, *others):
    count, width = rows.shape
    units = gate_mat.shape[1]
    depth = 1024

    def body(rows_ref, gate_ref, up_ref, *refs):
        gate_out, up_out, act_out = refs[-3:]
        step = pl.program_id(0)

        @pl.when(step == 0)
        def _():
            gate_out[...] = jnp.zeros_like(gate_out)
            up_out[...] = jnp.zeros_like(up_out)

        gate_out[...] += jnp.dot(rows_ref[...], gate_ref[...], preferred_element_type=F32)
        up_out[...] += jnp.dot(rows_ref[...], up_ref[...], preferred_element_type=F32)

        @pl.when(step == pl.num_programs(0) - 1)
        def _():
            gate = gate_out[...]
            act_out[...] = (gate * jax.nn.sigmoid(gate) * up_out[...]).astype(BF)

    whole = pl.BlockSpec((count, units), lambda k: (0, 0))
    weight = pl.BlockSpec((depth, units), lambda k: (k, 0))
    return pl.pallas_call(
        body,
        grid=(width // depth,),
        out_shape=[
            jax.ShapeDtypeStruct((count, units), F32),
            jax.ShapeDtypeStruct((count, units), F32),
            jax.ShapeDtypeStruct((count, units), BF),
        ],
        in_specs=[pl.BlockSpec((count, depth), lambda k: (0, k)), weight, weight]
        + [ANYWHERE] * len(others),
        out_specs=[whole, whole, whole],
        compiler_params=params(),
    )(rows, gate_mat, up_mat, *others)


def backward_far(here, h, gate_pre, up_proj, act, grad_inner, gate_mat, up_mat, *others):
    count, units = gate_pre.shape
    experts, capacity, _ = grad_inner.shape
    quarter = gate_mat.shape[0] // 4
    block = quarter // 2
    half = count // 2

    def body(here_ref, gate_pre_ref, up_ref, act_ref, inner_ref, gate_w, up_w, *refs):
        ggp, gup, low, high = refs[-4:]

        @pl.when(pl.program_id(0) == 0)
        def _():
            inner = inner_ref[...].reshape(count, units)
            gate = gate_pre_ref[...]
            sig = jax.nn.sigmoid(gate)
            ggp[...] = (inner * up_ref[...] * sig * (1.0 + gate * (1.0 - sig))).astype(BF)
            gup[...] = (inner * gate * sig).astype(BF)
            for out in (low, high):
                out[:, :units] = act_ref[:half]
                out[:, units : 2 * units] = act_ref[half:]

        piece = dot(ggp[...], gate_w[...], ((1,), (1,))) + dot(gup[...], up_w[...], ((1,), (1,)))
        for j in range(2):

            @pl.when(pl.program_id(0) == j)
            def _():
                columns = slice(2 * units + j * block, 2 * units + (j + 1) * block)
                low[:, columns] = piece[:half].astype(BF)
                high[:, columns] = piece[half:].astype(BF)

    whole = pl.BlockSpec((count, units), lambda j, here: (0, 0))
    weight = pl.BlockSpec((block, units), lambda j, here: (((here[0] + 2) % 4) * 2 + j, 0))
    out = pl.BlockSpec((half, 2 * units + quarter), lambda j, here: (0, 0))
    return pl.pallas_call(
        body,
        grid_spec=pltpu.PrefetchScalarGridSpec(
            num_scalar_prefetch=1,
            grid=(2,),
            in_specs=[
                whole,
                whole,
                whole,
                pl.BlockSpec((experts, capacity // 2, units), lambda j, here: (0, h, 0)),
                weight,
                weight,
            ]
            + [ANYWHERE] * len(others),
            out_specs=[whole, whole, out, out],
        ),
        out_shape=[
            jax.ShapeDtypeStruct((count, units), BF),
            jax.ShapeDtypeStruct((count, units), BF),
            jax.ShapeDtypeStruct((half, 2 * units + quarter), BF),
            jax.ShapeDtypeStruct((half, 2 * units + quarter), BF),
        ],
        compiler_params=params(),
    )(here, gate_pre, up_proj, act, grad_inner, gate_mat, up_mat, *others)


def backward_rest(here, grad_gate_pre, grad_up, gate_mat, up_mat):
    count, units = grad_up.shape
    quarter = gate_mat.shape[0] // 4
    block = quarter // 2

    def body(here_ref, ggp, gup, gate_w, up_w, *outs):
        step = pl.program_id(0)
        piece = dot(ggp[...], gate_w[...], ((1,), (1,))) + dot(gup[...], up_w[...], ((1,), (1,)))
        piece = piece.astype(BF)
        for i in range(3):

            @pl.when(step // 2 == i)
            def _():
                outs[i][...] = piece

    whole = pl.BlockSpec((count, units), lambda s, here: (0, 0))

    def weight_block(s, here):
        r = jnp.where(s // 2 == 0, 1, jnp.where(s // 2 == 1, 3, 0))
        return (((here[0] + r) % 4) * 2 + s % 2, 0)

    def out_spec(i):
        return pl.BlockSpec((count, block), lambda s, here: (0, jnp.clip(s - 2 * i, 0, 1)))

    weight = pl.BlockSpec((block, units), weight_block)
    return pl.pallas_call(
        body,
        grid_spec=pltpu.PrefetchScalarGridSpec(
            num_scalar_prefetch=1,
            grid=(6,),
            in_specs=[whole, whole, weight, weight],
            out_specs=[out_spec(i) for i in range(3)],
        ),
        out_shape=[jax.ShapeDtypeStruct((count, quarter), BF) for _ in range(3)],
        compiler_params=params(),
    )(here, grad_gate_pre, grad_up, gate_mat, up_mat)


def down_product(acts, downs, *others):
    count, units = acts[0].shape
    quarter = downs[0].shape[1]
    block = 256
    half_units = units // 2

    def body(a0, a1, a3, a2_low, a2_high, *refs):
        down_refs, (out, above, below, far) = refs[: len(downs)], refs[-4:]

        @pl.when(pl.program_id(0) == 0)
        def _():
            for act, rows in ((a2_low, pl.ds(0, count // 2)), (a2_high, pl.ds(count // 2, count // 2))):
                if act.shape[0] == count:
                    far[rows, :half_units] = act[: count // 2]
                    far[rows, half_units:] = act[count // 2 :]
                else:
                    far[rows, :] = act[...]
            for act, full in ((a1, above), (a3, below)):
                full[: count // 2] = act[:, :units]
                full[count // 2 :] = act[:, units : 2 * units]

        total = jnp.dot(a0[...], down_refs[0][...], preferred_element_type=F32)
        total += jnp.dot(above[...], down_refs[1][...], preferred_element_type=F32)
        total += jnp.dot(below[...], down_refs[2][...], preferred_element_type=F32)
        start = 0
        for piece, ref in zip(downs[3:], down_refs[3:]):
            left = far[:, start : start + piece.shape[0]]
            total += jnp.dot(left, ref[...], preferred_element_type=F32)
            start += piece.shape[0]
        out[...] = total.astype(BF)

    def held(array):
        return pl.BlockSpec(array.shape, lambda j: (0, 0))

    def streamed(array):
        return pl.BlockSpec((array.shape[0], block), lambda j: (0, j))

    return pl.pallas_call(
        body,
        grid=(quarter // block,),
        out_shape=jax.ShapeDtypeStruct((count, 2 * quarter), BF),
        in_specs=[held(acts[0])]
        + [pl.BlockSpec((count // 2, 2 * units), lambda j: (0, 0))] * 2
        + [
            held(a) if a.shape[1] == units else pl.BlockSpec((count, half_units), lambda j: (0, 0))
            for a in acts[3:]
        ]
        + [streamed(d) for d in downs]
        + [ANYWHERE] * len(others),
        out_specs=pl.BlockSpec((count, block), lambda j: (0, j)),
        scratch_shapes=[pltpu.VMEM((count, units), BF)] * 3,
        compiler_params=params(),
    )(*acts, *downs, *others)


def exchange(value):
    return lax.all_to_all(value, "ep", split_axis=0, concat_axis=0, tiled=True)


def per_device(
    hidden_rows,
    emb_rows,
    expert_ids,
    gate_scores,
    gain_hidden,
    gain_emb,
    gate_weight,
    up_weight,
    down_weight,
    output_grad,
):
    tokens, width = hidden_rows.shape
    quarter = emb_rows.shape[1]
    routes = expert_ids.shape[1]
    experts = lax.axis_size("ep")
    ring = lax.axis_size("pp")
    here = lax.axis_index("pp")
    capacity = 2 * tokens * routes // experts
    part = capacity // 2
    gate_mat, up_mat, down_mat = gate_weight[0], up_weight[0], down_weight[0]
    hidden_units = down_mat.shape[0]

    def columns(array, r):
        return lax.dynamic_slice_in_dim(array, ((here + r) % ring) * quarter, quarter, 1)

    flat_ids = expert_ids.reshape(-1)
    onehot = (flat_ids[:, None] == jnp.arange(experts, dtype=jnp.int32)[None, :]).astype(jnp.int32)
    ranking = jnp.sum(jnp.cumsum(onehot, axis=0) * onehot, axis=1) - 1
    ranking = ranking.reshape(tokens, routes)
    slot_ids = expert_ids * capacity + ranking
    slot_range = jnp.arange(experts * capacity, dtype=jnp.int32)
    selectors = [slot_ids[:, k][:, None] == slot_range[None, :] for k in range(routes)]
    placement = (selectors[0] | selectors[1]).astype(BF)
    slot_score = jnp.sum(
        sum(selectors[k].astype(F32) * gate_scores[:, k : k + 1] for k in range(routes)), axis=0
    )
    part_ids = jnp.where(
        ranking < part,
        expert_ids * part + ranking,
        experts * part + expert_ids * part + ranking - part,
    )
    part_range = jnp.arange(experts * part, dtype=jnp.int32)
    part_selectors = [
        [part_ids[:, k][:, None] == (part_range + h * experts * part)[None, :] for k in range(routes)]
        for h in range(2)
    ]
    part_placement = [(part_selectors[h][0] | part_selectors[h][1]).astype(BF) for h in range(2)]

    emb_own, emb_above, emb_below, emb_low, emb_high = ring_gather(emb_rows)
    emb_pieces = [emb_own, emb_above, jnp.concatenate([emb_low, emb_high], axis=0), emb_below]

    place = here.reshape(1)
    fourth = hidden_units // 4
    down_far = [cut_columns(place, down_mat, 2, i * fourth, fourth) for i in range(4)]
    ways = (1, 1, -1, -1)
    passing = [None] * 4
    for i in (0, 2, 1, 3):
        passing[i] = shift(down_far[i], ways[i])
    far_pieces = [shift(passing[i], ways[i]) for i in range(4)]

    grad_send = (dot(placement, output_grad, ((0,), (0,))) * slot_score[:, None]).astype(BF)
    grad_send = after(grad_send, *down_far)
    grad_slots = exchange(grad_send.reshape(experts, capacity, quarter))
    grad_slots = grad_slots.reshape(experts * capacity, quarter)

    emb_twice = jnp.concatenate(emb_pieces + emb_pieces, axis=1)
    emb_full = lax.dynamic_slice_in_dim(emb_twice, ((ring - here) % ring) * quarter, width, 1)
    hidden_f = hidden_rows.astype(F32)
    emb_f = emb_full.astype(F32)
    hidden_scale = jnp.sqrt(jnp.mean(hidden_f * hidden_f, axis=1, keepdims=True) + EPS)
    emb_scale = jnp.sqrt(jnp.mean(emb_f * emb_f, axis=1, keepdims=True) + EPS)
    mixed_input = (hidden_f / hidden_scale * gain_hidden + emb_f / emb_scale * gain_emb).astype(BF)
    send_rows = [
        dot(part_placement[h], mixed_input, ((0,), (0,))).astype(BF) for h in range(2)
    ]
    down_up = cut_columns(place, down_mat, 1, 0, hidden_units, passing[0])
    down_back = cut_columns(place, down_mat, 3, 0, hidden_units, passing[0])
    down_below, down_above = shift(down_up, 1), shift(down_back, -1)
    down_own = cut_columns(place, down_mat, 0, 0, hidden_units, grad_slots)
    far = inner_share(grad_slots, far_pieces)
    own = dot(grad_slots, down_own, ((1,), (1,)))
    send_rows[0] = after(
        send_rows[0], *passing, far_pieces[0], far_pieces[2], down_up, down_back
    )
    send_rows[1] = after(send_rows[1], *far, own)
    arrived = [
        exchange(send_rows[h].reshape(experts, part, width)).reshape(experts * part, width)
        for h in range(2)
    ]
    downs = (down_own, down_above, down_below, *far_pieces)
    up = jnp.concatenate(inner_share(grad_slots, (down_above,)), axis=0)
    down = jnp.concatenate(inner_share(grad_slots, (down_below,)), axis=0)
    came = shift(far[0], 1), shift(far[1], -1)
    inner_shares, passed = ring_scatter(*came, (up, down, own))

    for h in range(2):
        gate_pre, up_proj, act = forward(arrived[h], gate_mat, up_mat, *passed)
        if h == 0:
            inner_shares = (after(own, act), *inner_shares[1:])
            grad_inner = sum(share.astype(F32) for share in inner_shares)
            grad_inner = grad_inner.reshape(experts, capacity, hidden_units)
        grad_gate_pre, grad_up, low, high = backward_far(
            place, h, gate_pre, up_proj, act, grad_inner, gate_mat, up_mat
        )
        below, above = shift(low, 1), shift(high, -1)
        rest = backward_rest(place, grad_gate_pre, grad_up, gate_mat, up_mat)
        if h == 0:
            shares, passed = ring_scatter(below, above, rest, carry=True)
            act_low, act_high = shares[1], shares[2]
            first = (act, above, below, act_low, act_high), shares
    first_output = down_product(first[0], downs, low)
    act_low = shift(carried(below, 0, hidden_units, rest[0]), 1)
    act_high = shift(carried(above, 1, hidden_units, rest[0]), -1)
    second, passed = ring_scatter(below, above, rest, act_low, act_high)
    output = down_product((act, above, below, act_low, act_high), downs, *passed)
    returned = [
        exchange(both.reshape(experts, part, 2 * quarter))
        for both in (
            sum_beside(first_output, first[1], below, above, rest[0]),
            sum_beside(output, second),
        )
    ]
    returned = [both.reshape(experts * part, 2 * quarter) for both in returned]
    back = [both[:, :quarter] for both in returned]
    grads_back = [both[:, quarter:] for both in returned]

    route_outputs = [
        sum(dot(part_selectors[h][k].astype(BF), back[h], ((1,), (0,))) for h in range(2))
        for k in range(routes)
    ]
    moe_out = sum(gate_scores[:, k : k + 1] * route_outputs[k] for k in range(routes)).astype(BF)
    input_grad = sum(dot(part_placement[h], grads_back[h], ((1,), (0,))) for h in range(2))

    grad_f = output_grad.astype(F32)
    hidden_cols = columns(hidden_rows, 0).astype(F32)
    emb_cols = emb_rows.astype(F32)
    gain_hidden_cols = lax.dynamic_slice_in_dim(gain_hidden, here * quarter, quarter, 0)
    gain_emb_cols = lax.dynamic_slice_in_dim(gain_emb, here * quarter, quarter, 0)
    partial = jnp.stack(
        [jnp.sum(grad_f * route_outputs[k], axis=1) for k in range(routes)]
        + [
            jnp.sum(input_grad * gain_hidden_cols * hidden_cols, axis=1),
            jnp.sum(input_grad * gain_emb_cols * emb_cols, axis=1),
        ],
        axis=0,
    )
    total = partial + shift(partial, 1) + shift(partial, 2) + shift(partial, 3)
    grad_gate = total[:routes].T
    hidden_dot, emb_dot = total[routes][:, None], total[routes + 1][:, None]
    hidden_cube = hidden_scale * hidden_scale * hidden_scale
    emb_cube = emb_scale * emb_scale * emb_scale
    grad_hidden = gain_hidden_cols * input_grad / hidden_scale - hidden_cols * hidden_dot / (
        width * hidden_cube
    )
    grad_emb = gain_emb_cols * input_grad / emb_scale - emb_cols * emb_dot / (width * emb_cube)
    return moe_out, grad_gate, grad_hidden.astype(BF), grad_emb.astype(BF)


def solution(mesh):
    in_specs = (
        P("ep", None),
        P("ep", "pp"),
        P("ep", None),
        P("ep", None),
        P(),
        P(),
        P("ep", None, "pp"),
        P("ep", None, "pp"),
        P("ep", "pp", None),
        P("ep", "pp"),
    )
    out_specs = (P("ep", "pp"), P("ep", None), P("ep", "pp"), P("ep", "pp"))
    return jax.shard_map(
        per_device, mesh=mesh, in_specs=in_specs, out_specs=out_specs, check_vma=False
    )
```
